256 devices in a mesh: batch: 8 (over z), tm: 8 (over x, y_lo), space: 4 (over y_hi, core).
Axes of the slice: x: 4, y: 4 (y_hi: 2, y_lo: 2; y = y_hi * 2 + y_lo), z: 8, core: 2. Of those that a mesh axis runs over, the one named last changes fastest.
Arguments:
- video: bfloat16 [16, 32, 16, 16, 1024], P('batch', 'tm', 'space'), may hold values from -8 to 8
- shifts: int32 [16, 3], P('batch'), may hold values from -4 to 4, as said below
- head_scale: float32 [16], replicated, may hold values from 4 to 16
- w_qkv: bfloat16 [1024, 3072], replicated, may hold values from -0.1875 to 0.1875
- w_out: bfloat16 [1024, 1024], replicated, may hold values from -0.1875 to 0.1875
- w_emb: bfloat16 [1024, 768], replicated, may hold values from -0.1875 to 0.1875
- text: bfloat16 [16, 768], P('batch'), may hold values from -0.21875 to 0.21875
- bucket: int32 [16, 16], P('batch'), may hold values from 0 to 3
- bucket_scale: float32 [4], replicated, may hold values from 0.25 to 4
Outputs:
- video_grad: bfloat16 [16, 32, 16, 16, 1024], P('batch', 'tm', 'space')
- text_grad: float32 [16, 768], P('batch')
- contrast_loss: float32 [], replicated
The draws below stay inside these ranges and needn't reach their ends.
Inputs may be any that keep to these rules, and one draw needn't show every extreme that they name: `shifts`: columns 0 and 1 of the shift of clip c are nonzero and at most 2 in magnitude, positive for even c and negative for odd c; column 2 is at most 4 in magnitude.
All inputs are finite; a program needn't handle non-finite values.
Results may differ from the reference program's by a relative error of at most 0.015.
Values may be sent and summed in bfloat16 or wider, within the bound.
No kernel may reach another device: no remote copies, remote signals or barrier semaphores. Data moves between devices by JAX's collectives and lax.ppermute only.
A program may use at most 128 MiB of HBM per device.

```python
import math
import jax
import jax.numpy as jnp
from jax import lax

HEADS = 16
HEAD_DIM = 64
D = 1024
EMB = 768
ROWS = 16
COLS = 16
WT = 4
WH = 4
WW = 8
HALO = 2
NBUCK = 4
CLIPS = 16
FRAMES = 32


def draw_shifts(key, part):
    key = jax.random.fold_in(key, 11)
    subkeys = jax.random.split(key, 4)
    half_count = CLIPS // 2
    magnitude = jax.random.randint(subkeys[0], (CLIPS, 2), 1, HALO + 1)
    even_pick = 2 * jax.random.randint(subkeys[1], (), 0, half_count)
    odd_pick = 2 * jax.random.randint(subkeys[2], (), 0, half_count) + 1
    magnitude = magnitude.at[even_pick].set(HALO).at[odd_pick].set(HALO)
    parity = jnp.arange(CLIPS) % 2
    signed = magnitude * (1 - 2 * parity)[:, None]
    across = jax.random.randint(subkeys[3], (CLIPS,), -(WW // 2), WW // 2 + 1)
    across = across.at[even_pick].set(WW // 2).at[odd_pick].set(-(WW // 2))
    return jnp.concatenate([signed, across[:, None]], axis=1).astype(jnp.int32)


def draw_video(key, part):
    key = jax.random.fold_in(key, 12)
    subkeys = jax.random.split(key, 1)
    full_shape = (CLIPS, FRAMES, ROWS, COLS, D)
    frame_ramp = 1.0 + 2.0 * jnp.arange(FRAMES, dtype=jnp.float32) / (FRAMES - 1)
    frame_ramp = frame_ramp[None, :, None, None, None]
    values = jnp.clip(jax.random.normal(subkeys[0], full_shape), -6.0, 6.0) * frame_ramp
    return jnp.clip(values, -8.0, 8.0).astype(jnp.bfloat16)


def place_ends(array, stream_key, least, largest):
    longest = array.shape.index(max(array.shape))
    spots = []
    for shift in (0, 1):
        where = [jax.random.randint(jax.random.fold_in(stream_key, axis), (), 0, length) for axis, length in enumerate(array.shape)]
        where[longest] = (where[longest] + shift) % array.shape[longest]
        spots.append(tuple(where))
    return array.at[spots[0]].set(least).at[spots[1]].set(largest)


def block_levels(own_key, dims, cuts, smallest, top_value):
    factor_of = 1.0
    for axis_at, shards_of in cuts:
        steps = jax.random.uniform(jax.random.fold_in(jax.random.fold_in(own_key, 6), axis_at), (shards_of,), jnp.float32, smallest / len(cuts), top_value / len(cuts))
        factor_of = factor_of * jnp.repeat(jnp.exp(steps), dims[axis_at] // shards_of).reshape((-1,) + (1,) * (len(dims) - 1 - axis_at))
    return factor_of


def bell_draw(rng, dims, scale, most, pieces=(), kind=jnp.bfloat16):
    entries = scale * jax.random.normal(rng, dims, jnp.float32)
    if pieces:
        entries = entries * block_levels(rng, dims, pieces, -0.22, 0.18)
    return jnp.clip(entries, -most, most).astype(kind)


def setup_inputs(seed: int = 0) -> dict:
    key_of = jax.random.split(jax.random.key(seed), 10)
    video = draw_video(jax.random.fold_in(key_of[9], 71), 0)
    shifts = draw_shifts(jax.random.fold_in(key_of[9], 71), 0)
    head_scale = jnp.clip(jnp.exp(jax.random.uniform(key_of[2], (HEADS,), jnp.float32, math.log(4.0), math.log(16.0))), 4.0, 16.0)
    w_qkv = bell_draw(key_of[3], (D, 3 * D), D ** -0.5, 0.1875)
    w_out = bell_draw(key_of[4], (D, D), D ** -0.5, 0.1875)
    w_emb = bell_draw(key_of[5], (D, EMB), D ** -0.5, 0.1875)
    text = bell_draw(key_of[6], (CLIPS, EMB), EMB ** -0.5, 0.21875, ((0, 8),))
    bucket = place_ends(jax.random.randint(key_of[7], (CLIPS, CLIPS), 0, NBUCK), jax.random.fold_in(key_of[7], 1), 0, NBUCK - 1).astype(jnp.int32)
    bucket_scale = jnp.clip(jnp.exp(jax.random.uniform(key_of[8], (NBUCK,), jnp.float32, math.log(0.25), math.log(4.0))), 0.25, 4.0)
    return dict(video=video, shifts=shifts, head_scale=head_scale, w_qkv=w_qkv, w_out=w_out, w_emb=w_emb, text=text, bucket=bucket, bucket_scale=bucket_scale)


SOFTMAX_TEMP = 0.07
NORM_EPS = 1e-05
QUERY_EPS = 1e-06
EMBED_EPS = 1e-06
PRECISE_MATMUL = lax.Precision.HIGHEST

def outside_range(position, offset, extent):
    moved = position + offset
    return jnp.logical_or(moved < 0, moved >= extent).astype(jnp.int32)

def region_labels(frame_pos, row_pos, column_pos, offset, frame_extent, row_extent, column_extent):
    first_label = outside_range(frame_pos, offset[0], frame_extent)
    second_label = outside_range(row_pos, offset[1], row_extent)
    third_label = outside_range(column_pos, offset[2], column_extent)
    return first_label[:, None, None] * 4 + second_label[None, :, None] * 2 + third_label[None, None, :]

def window_split(blocks):
    clips_here, frames, row_count, columns, feature_dim = blocks.shape
    tiled = blocks.reshape(clips_here, frames // WT, WT, row_count // WH, WH, columns // WW, WW, feature_dim)
    tiled = tiled.transpose(0, 1, 3, 5, 2, 4, 6, 7)
    return tiled.reshape(-1, WT * WH * WW, feature_dim)

def window_merge(tiles, clips_here, frames, row_count, columns):
    feature_dim = tiles.shape[-1]
    tiled = tiles.reshape(clips_here, frames // WT, row_count // WH, columns // WW, WT, WH, WW, feature_dim)
    tiled = tiled.transpose(0, 1, 4, 2, 5, 3, 6, 7)
    return tiled.reshape(clips_here, frames, row_count, columns, feature_dim)

def attend_forward(blocks, labels, w_qkv, head_scale):
    tiles = window_split(blocks)
    marks = window_split(labels[..., None])[..., 0]
    win_count, win_size, model_width = tiles.shape
    wide = tiles.astype(jnp.float32)
    centered = wide - lax.optimization_barrier(jnp.mean(wide, axis=-1, keepdims=True))
    inv_std = lax.rsqrt(lax.optimization_barrier(jnp.mean(centered * centered, axis=-1, keepdims=True)) + NORM_EPS)
    normed = centered * inv_std
    flat = normed.astype(jnp.bfloat16).reshape(win_count * win_size, model_width)
    projected = jnp.dot(flat, w_qkv, preferred_element_type=jnp.float32)
    projected = projected.reshape(win_count, win_size, 3, HEADS, HEAD_DIM)
    query = projected[:, :, 0]
    key_part = projected[:, :, 1]
    value_part = projected[:, :, 2]
    q_norm = jnp.sqrt(lax.optimization_barrier(jnp.sum(query * query, axis=-1, keepdims=True)) + QUERY_EPS)
    k_norm = jnp.sqrt(lax.optimization_barrier(jnp.sum(key_part * key_part, axis=-1, keepdims=True)) + QUERY_EPS)
    q_unit = query / q_norm
    k_unit = key_part / k_norm
    q_low = q_unit.astype(jnp.bfloat16)
    k_low = k_unit.astype(jnp.bfloat16)
    v_low = value_part.astype(jnp.bfloat16)
    scores = jnp.einsum('wqhe,wkhe->whqk', q_low.astype(jnp.float32), k_low.astype(jnp.float32), precision=PRECISE_MATMUL)
    scores = scores * head_scale[None, :, None, None]
    same = (marks[:, :, None] == marks[:, None, :])[:, None]
    exp_score = jnp.where(same, jnp.exp(scores), 0.0)
    prob = exp_score / lax.optimization_barrier(jnp.sum(exp_score, axis=-1, keepdims=True))
    prob_low = prob.astype(jnp.bfloat16)
    mixed = jnp.einsum('whqk,wkhe->wqhe', prob_low.astype(jnp.float32), v_low.astype(jnp.float32), precision=PRECISE_MATMUL)
    out_low = mixed.reshape(win_count, win_size, model_width).astype(jnp.bfloat16)
    stored = (normed, inv_std, q_unit, k_unit, q_norm, k_norm, q_low, k_low, v_low, prob, prob_low)
    return (stored, out_low)

def attend_backward(stored, clip_rows, out_rows, w_qkv, head_scale):
    normed, inv_std, q_unit, k_unit, q_norm, k_norm, q_low, k_low, v_low, prob, prob_low = stored
    win_count, win_size, model_width = normed.shape
    d_heads = out_rows.astype(jnp.float32).reshape(win_count, HEADS, HEAD_DIM)
    along = jnp.einsum('whe,wkhe->whk', d_heads, v_low.astype(jnp.float32), precision=PRECISE_MATMUL)
    inner = lax.optimization_barrier(jnp.sum(prob * along[:, :, None, :], axis=-1, keepdims=True))
    d_score = (prob * (along[:, :, None, :] - inner)).astype(jnp.bfloat16).astype(jnp.float32)
    scale = head_scale[None, None, :, None]
    dq_unit = jnp.einsum('whqk,wkhe->wqhe', d_score, k_low.astype(jnp.float32), precision=PRECISE_MATMUL) * scale
    dk_unit = jnp.einsum('whqk,wqhe->wkhe', d_score, q_low.astype(jnp.float32), precision=PRECISE_MATMUL) * scale
    mass = lax.optimization_barrier(jnp.sum(prob_low.astype(jnp.float32), axis=2))
    d_values = jnp.transpose(mass, (0, 2, 1))[..., None] * d_heads[:, None]
    d_query = (dq_unit - q_unit * lax.optimization_barrier(jnp.sum(q_unit * dq_unit, axis=-1, keepdims=True))) / q_norm
    d_keys = (dk_unit - k_unit * lax.optimization_barrier(jnp.sum(k_unit * dk_unit, axis=-1, keepdims=True))) / k_norm
    d_projected = jnp.stack([d_query, d_keys, d_values], axis=2)
    d_projected = d_projected.reshape(win_count * win_size, 3 * model_width).astype(jnp.bfloat16)
    d_normed = jnp.dot(d_projected, w_qkv.T, preferred_element_type=jnp.float32)
    d_normed = d_normed.reshape(win_count, win_size, model_width)
    first_mean = lax.optimization_barrier(jnp.mean(d_normed, axis=-1, keepdims=True))
    second_mean = lax.optimization_barrier(jnp.mean(d_normed * normed, axis=-1, keepdims=True))
    d_tokens = inv_std * (d_normed - first_mean - normed * second_mean)
    return (clip_rows[:, None, :] + d_tokens).astype(jnp.bfloat16)

def full_contrast(similarity_logits, weights):
    pair_count = similarity_logits.shape[0]
    own_pair = jnp.eye(pair_count, dtype=bool)
    exp_logit = jnp.exp(similarity_logits)
    negative = jnp.where(own_pair, 0.0, weights * exp_logit)
    other_weight = jnp.where(own_pair, 0.0, weights)
    self_logit = lax.optimization_barrier(jnp.sum(jnp.where(own_pair, similarity_logits, 0.0), axis=1))
    self_exp = jnp.exp(self_logit)
    row_weight = lax.optimization_barrier(jnp.sum(other_weight, axis=1))
    column_weight = lax.optimization_barrier(jnp.sum(other_weight, axis=0))
    row_partition = self_exp + (pair_count - 1) * lax.optimization_barrier(jnp.sum(negative, axis=1)) / row_weight
    column_partition = self_exp + (pair_count - 1) * lax.optimization_barrier(jnp.sum(negative, axis=0)) / column_weight
    summed = jnp.sum(jnp.log(row_partition) - self_logit) + jnp.sum(jnp.log(column_partition) - self_logit)
    scaled = (pair_count - 1) * weights * exp_logit
    off_grad = scaled * (1.0 / (row_weight * row_partition))[:, None] + scaled * (1.0 / (column_weight * column_partition))[None, :]
    on_grad = self_exp / row_partition - 1.0 + self_exp / column_partition - 1.0
    logit_gradient = jnp.where(own_pair, on_grad[:, None], off_grad)
    return (summed / (2 * pair_count), logit_gradient)

def reference(video, shifts, head_scale, w_qkv, w_out, w_emb, text, bucket, bucket_scale):
    clip_tokens = FRAMES * ROWS * COLS
    frame_pos = jnp.arange(FRAMES, dtype=jnp.int32)
    row_pos = jnp.arange(ROWS, dtype=jnp.int32)
    column_pos = jnp.arange(COLS, dtype=jnp.int32)

    def forward_one(block, offset):
        rolled = jnp.roll(block, -offset, axis=(0, 1, 2))
        labels = region_labels(frame_pos, row_pos, column_pos, offset, FRAMES, ROWS, COLS)
        return attend_forward(rolled[None], labels[None], w_qkv, head_scale)

    def forward_sums(items):
        block, offset = items
        stored, out_low = forward_one(block, offset)
        return lax.optimization_barrier(jnp.sum(out_low.astype(jnp.float32), axis=(0, 1)))
    out_total = lax.map(forward_sums, (video, shifts))
    token_total = lax.optimization_barrier(jnp.sum(video.astype(jnp.float32), axis=(1, 2, 3)))
    out_mean = (out_total / clip_tokens).astype(jnp.bfloat16)
    pooled = token_total / clip_tokens + jnp.dot(out_mean, w_out, preferred_element_type=jnp.float32)
    embedded = jnp.dot(pooled.astype(jnp.bfloat16), w_emb, preferred_element_type=jnp.float32)
    emb_norm = jnp.sqrt(lax.optimization_barrier(jnp.sum(embedded * embedded, axis=-1, keepdims=True)) + EMBED_EPS)
    clip_unit_vector = embedded / emb_norm
    text_wide = text.astype(jnp.float32)
    text_norm = jnp.sqrt(lax.optimization_barrier(jnp.sum(text_wide * text_wide, axis=-1, keepdims=True)) + EMBED_EPS)
    text_unit_vector = text_wide / text_norm
    similarity_logits = jnp.dot(clip_unit_vector, text_unit_vector.T, precision=PRECISE_MATMUL) / SOFTMAX_TEMP
    levels = jnp.arange(bucket_scale.shape[0], dtype=jnp.int32)
    weights = lax.optimization_barrier(jnp.sum(jnp.where(bucket[..., None] == levels, bucket_scale, 0.0), axis=-1))
    contrast_loss, logit_gradient = full_contrast(similarity_logits, weights)
    clip_gradient = jnp.dot(logit_gradient, text_unit_vector, precision=PRECISE_MATMUL) / SOFTMAX_TEMP
    text_gradient = jnp.dot(logit_gradient.T, clip_unit_vector, precision=PRECISE_MATMUL) / SOFTMAX_TEMP
    text_grad = (text_gradient - text_unit_vector * lax.optimization_barrier(jnp.sum(text_unit_vector * text_gradient, axis=-1, keepdims=True))) / text_norm
    d_embed = (clip_gradient - clip_unit_vector * lax.optimization_barrier(jnp.sum(clip_unit_vector * clip_gradient, axis=-1, keepdims=True))) / emb_norm
    clip_grad = jnp.dot(d_embed, w_emb.astype(jnp.float32).T, precision=PRECISE_MATMUL)
    d_out = jnp.dot(clip_grad, w_out.astype(jnp.float32).T, precision=PRECISE_MATMUL).astype(jnp.bfloat16)

    def backward_one(items):
        block, offset, grad_row, out_row = items
        stored, out_low = forward_one(block, offset)
        win_count = out_low.shape[0]
        clip_rows = jnp.broadcast_to(grad_row, (win_count, grad_row.shape[0]))
        out_rows = jnp.broadcast_to(out_row, (win_count, out_row.shape[0]))
        d_tiles = attend_backward(stored, clip_rows, out_rows, w_qkv, head_scale)
        d_rolled = window_merge(d_tiles, 1, FRAMES, ROWS, COLS)[0]
        return jnp.roll(d_rolled, offset, axis=(0, 1, 2))
    video_grad = lax.map(backward_one, (video, shifts, clip_grad, d_out))
    return (video_grad, text_grad, contrast_loss)
```

```python
from functools import partial

import jax
import jax.numpy as jnp
from jax import lax
from jax.experimental import pallas as pl
from jax.experimental.pallas import tpu as pltpu
from jax.sharding import PartitionSpec as P

HEADS = 16
HEAD_DIM = 64
D = 1024
EMB = 768
WT = 4
WH = 4
WW = 8
COLS = 16
HALO = 2
TOK = WT * WH * WW
QUADS = 4
QW = 256

SOFTMAX_TEMP = 0.07
NORM_EPS = 1e-05
QUERY_EPS = 1e-06
EMBED_EPS = 1e-06
LOG2E = 1.4426950408889634
F32 = jnp.float32
BF16 = jnp.bfloat16
VMEM_LIMIT = 56 * 1024 * 1024

NT = (((1,), (1,)), ((), ()))
TN = (((0,), (0,)), ((), ()))

GRID = 6
OWN = ((0, 4, 0, 4), (2, 4, 2, 4))
PIECES = (
    ((4, 2, 1, 3), (1, 3, 4, 2), (4, 2, 4, 2)),
    ((0, 2, 2, 3), (2, 3, 0, 2), (0, 2, 0, 2)),
)
GIVEN = (
    ((0, 2, 1, 3), (1, 3, 0, 2), (0, 2, 0, 2)),
    ((2, 2, 0, 3), (0, 3, 2, 2), (2, 2, 2, 2)),
)
PIECE_SHAPES = tuple((g[1], g[3], COLS, D) for g in GIVEN[0])


def vmem():
    return pl.BlockSpec(memory_space=pltpu.VMEM)


def smem():
    return pl.BlockSpec(memory_space=pltpu.SMEM)


def hbm():
    return pl.BlockSpec(memory_space=pl.ANY)


def whole(shape):
    return pl.BlockSpec(shape, lambda i: (0,) * len(shape))


def params(**more):
    return pltpu.CompilerParams(vmem_limit_bytes=VMEM_LIMIT, **more)


def pack_kernel(video, *refs):
    outs, sems = refs[:6], refs[6]
    copies = []
    for c in range(2):
        for k in range(3):
            f, nf, r, nr = GIVEN[c][k]
            copies.append(
                pltpu.make_async_copy(
                    video.at[c, pl.ds(f, nf), pl.ds(r, nr)], outs[3 * c + k], sems.at[3 * c + k]
                )
            )
    for copy in copies:
        copy.start()
    for copy in copies:
        copy.wait()


def pack(video):
    return pl.pallas_call(
        pack_kernel,
        out_shape=[jax.ShapeDtypeStruct(s, BF16) for s in PIECE_SHAPES * 2],
        in_specs=[hbm()],
        out_specs=[hbm()] * 6,
        scratch_shapes=[pltpu.SemaphoreType.DMA((6,))],
        compiler_params=params(),
        name="pack",
    )(video)


def exchange(pieces, clip, sign):
    tm, space = lax.axis_size("tm"), lax.axis_size("space")
    step = sign if clip == 0 else -sign
    out = []
    for piece, (dt, ds) in zip(pieces, ((step, 0), (0, step), (step, step))):
        pairs = [
            (t * space + s, ((t + dt) % tm) * space + (s + ds) % space)
            for t in range(tm)
            for s in range(space)
        ]
        out.append(lax.ppermute(piece, ("tm", "space"), pairs))
    return out


def head_blocks(shape, width):
    row = lax.broadcasted_iota(jnp.int32, shape, 0) // width
    lane = lax.broadcasted_iota(jnp.int32, shape, 1) // HEAD_DIM
    return (row == lane).astype(F32).astype(BF16)


def low_lanes(shape):
    return lax.broadcasted_iota(jnp.int32, shape, 1) < HEAD_DIM


def split_heads(pair):
    low = low_lanes(pair.shape)
    wide = pair.astype(F32)
    return jnp.concatenate(
        [jnp.where(low, wide, 0.0), jnp.where(low, 0.0, wide)], axis=0
    ).astype(BF16)


def window_mask(frame0, row0, col0, s0, s1, s2, frames, rows):
    shape = (TOK, 2 * TOK)

    def label(index):
        f = frame0 + index // (WH * WW) + s0
        r = row0 + (index // WW) % WH + s1
        c = col0 + index % WW + s2
        one = lambda v, n: jnp.where((v < 0) | (v >= n), 1, 0)
        return one(f, frames) * 4 + one(r, rows) * 2 + one(c, COLS)

    key = lax.broadcasted_iota(jnp.int32, shape, 0)
    query = lax.broadcasted_iota(jnp.int32, shape, 1) % TOK
    return jnp.where(label(key) == label(query), 1.0, 0.0)


def forward_kernel(clips, frames, rows_all, pos, shifts, hscale, video, *refs):
    nc = len(clips)
    halo = refs[: 3 * nc]
    wq, wk, wv = refs[3 * nc : 3 * nc + 3]
    outs = refs[3 * nc + 3 :]
    ql, kl, vl, rq, rk, mass, prob, n32, istd, sums = outs[:10]
    ext, xb, masks, ones4, ones2, qs, ks = outs[10:]
    step = pl.program_id(0)

    @pl.when(step == 0)
    def _():
        ones4[...] = head_blocks((QW, QW), HEAD_DIM)
        ones2[...] = head_blocks((2 * TOK, 2 * HEAD_DIM), TOK)
        for n, c in enumerate(clips):
            f, nf, r, nr = OWN[c]
            ext[n, f : f + nf, r : r + nr] = video[n]
            for k in range(3):
                f, nf, r, nr = PIECES[c][k]
                ext[n, f : f + nf, r : r + nr] = halo[3 * n + k][...]
            s0, s1, s2 = shifts[c, 0], shifts[c, 1], shifts[c, 2]
            off0, off1 = s0 + HALO * c, s1 + HALO * c
            turn = (COLS - s2) % COLS

            def cells(a, total):
                for b in range(WH):
                    x = ext[n, a + off0, b + off1].astype(F32)
                    total = total + x
                    x = pltpu.roll(x, turn, 0)
                    centered = x - jnp.mean(x, axis=-1, keepdims=True)
                    inv = lax.rsqrt(
                        jnp.mean(centered * centered, axis=-1, keepdims=True) + NORM_EPS
                    )
                    y = centered * inv
                    wide = jnp.broadcast_to(inv, (COLS, 128))
                    for w in range(2):
                        start = pl.multiple_of(
                            (2 * n + w) * TOK + a * (WH * WW) + b * WW, WW
                        )
                        n32[pl.ds(start, WW)] = y[w * WW : (w + 1) * WW]
                        istd[pl.ds(start, WW)] = wide[w * WW : (w + 1) * WW]
                return total

            total = lax.fori_loop(0, WT, cells, jnp.zeros((COLS, D), F32))
            sums[2 * n : 2 * n + 1] = jnp.sum(total, axis=0, keepdims=True)
            for w in range(2):
                masks[2 * n + w] = window_mask(
                    pos[0] * WT, pos[1] * WH, w * WW, s0, s1, s2, frames, rows_all
                )
        xb[...] = n32[...].astype(BF16)

    x = xb[...]
    qs[...] = jnp.dot(x, wq[...], preferred_element_type=F32)
    ks[...] = jnp.dot(x, wk[...], preferred_element_type=F32)
    vl[...] = jnp.dot(x, wv[...], preferred_element_type=F32).astype(BF16)
    for full, unit, inverse in ((qs, ql, rq), (ks, kl, rk)):
        for w in range(2 * nc):
            at = slice(w * TOK, (w + 1) * TOK)
            value = full[at]
            square = jnp.dot(
                (value * value).astype(BF16), ones4[...], preferred_element_type=F32
            )
            inv = lax.rsqrt(square + QUERY_EPS)
            inverse[at] = inv
            unit[at] = (value * inv).astype(BF16)
    lane = lax.broadcasted_iota(jnp.int32, (1, 2 * TOK), 1)
    for p in range(2):
        head = step * 4 + 2 * p
        lanes = slice(p * 128, (p + 1) * 128)
        factor = jnp.where(lane < TOK, hscale[head], hscale[head + 1]) * LOG2E
        for n in range(nc):
            gathered = jnp.zeros((1, 128), F32)
            for w in range(2 * n, 2 * n + 2):
                at = slice(w * TOK, (w + 1) * TOK)
                score = lax.dot_general(
                    kl[at, lanes], split_heads(ql[at, lanes]), NT, preferred_element_type=F32
                )
                e = jnp.exp2(score * factor) * masks[w]
                pt = e * (1.0 / jnp.sum(e, axis=0, keepdims=True))
                prob[0, 2 * w + p] = pt
                held = jnp.dot(pt.astype(BF16), ones2[...], preferred_element_type=F32)
                mass[at, lanes] = held
                gathered = gathered + jnp.sum(
                    held * vl[at, lanes].astype(F32), axis=0, keepdims=True
                )
            start = pl.multiple_of(step * QW + p * 128, 128)
            sums[2 * n + 1 : 2 * n + 2, pl.ds(start, 128)] = gathered


def forward(clips, pos, shifts, hscale, video, halo, w_qkv):
    nc = len(clips)
    n = nc * 2 * TOK
    frames = lax.axis_size("tm") * WT
    rows_all = lax.axis_size("space") * WH
    first = clips[0] // nc
    column = lambda part: pl.BlockSpec((D, QW), lambda i: (0, part * QUADS + i))
    by_quad = lambda: pl.BlockSpec((n, QW), lambda i: (0, i))
    return pl.pallas_call(
        partial(forward_kernel, clips, frames, rows_all),
        grid=(QUADS,),
        out_shape=[jax.ShapeDtypeStruct((n, D), BF16)] * 3
        + [jax.ShapeDtypeStruct((n, D), F32)] * 3
        + [
            jax.ShapeDtypeStruct((QUADS, 4 * nc, TOK, 2 * TOK), F32),
            jax.ShapeDtypeStruct((n, D), F32),
            jax.ShapeDtypeStruct((n, 128), F32),
            jax.ShapeDtypeStruct((2 * nc, D), F32),
        ],
        in_specs=[smem(), smem(), smem()]
        + [pl.BlockSpec((nc, WT, WH, COLS, D), lambda i: (first, 0, 0, 0, 0))]
        + [whole(h.shape) for h in halo]
        + [column(0), column(1), column(2)],
        out_specs=[by_quad() for _ in range(6)]
        + [
            pl.BlockSpec((1, 4 * nc, TOK, 2 * TOK), lambda i: (i, 0, 0, 0)),
            whole((n, D)),
            whole((n, 128)),
            whole((2 * nc, D)),
        ],
        scratch_shapes=[
            pltpu.VMEM((nc, GRID, GRID, COLS, D), BF16),
            pltpu.VMEM((n, D), BF16),
            pltpu.VMEM((2 * nc, TOK, 2 * TOK), F32),
            pltpu.VMEM((QW, QW), BF16),
            pltpu.VMEM((2 * TOK, 2 * HEAD_DIM), BF16),
            pltpu.VMEM((n, QW), F32),
            pltpu.VMEM((n, QW), F32),
        ],
        compiler_params=params(dimension_semantics=("arbitrary",)),
        cost_estimate=pl.CostEstimate(
            flops=2 * n * D * 3 * D, bytes_accessed=12 * 2**20, transcendentals=n * 2048
        ),
        name="forward",
    )(pos, shifts, hscale, video, *halo, w_qkv, w_qkv, w_qkv)


def embed_kernel(tokens, got, w_out, w_emb, text, bucket, levels, out):
    total = jnp.sum(got[...], axis=0)
    mean = (jnp.concatenate([total[1:2], total[3:4]], axis=0) / tokens).astype(BF16)
    token_mean = jnp.concatenate([total[0:1], total[2:3]], axis=0) / tokens
    pooled = token_mean + jnp.dot(mean, w_out[...], preferred_element_type=F32)
    embedded = jnp.dot(pooled.astype(BF16), w_emb[...], preferred_element_type=F32)
    held = bucket[...]
    weight = jnp.zeros(held.shape, F32)
    for level in range(levels.shape[0]):
        weight = weight + jnp.where(held == level, levels[level], 0.0)
    weight = jnp.concatenate(
        [weight, jnp.zeros((held.shape[0], 128 - held.shape[1]), F32)], axis=1
    )
    words = text[...].astype(F32)
    block = jnp.concatenate(
        [
            jnp.concatenate([embedded, weight], axis=1),
            jnp.concatenate([words, jnp.zeros_like(weight)], axis=1),
        ],
        axis=0,
    )
    for peer in range(out.shape[0]):
        out[peer] = block


def embed(got, w_out, w_emb, text, bucket, levels, tokens, peers):
    return pl.pallas_call(
        partial(embed_kernel, tokens),
        out_shape=jax.ShapeDtypeStruct((peers, 4, EMB + 128), F32),
        in_specs=[vmem()] * 5 + [smem()],
        out_specs=vmem(),
        compiler_params=params(),
        name="embed",
    )(got, w_out, w_emb, text, bucket, levels)


def three_parts(wide):
    high = wide.astype(BF16)
    rest = wide - high.astype(F32)
    middle = rest.astype(BF16)
    low = (rest - middle.astype(F32)).astype(BF16)
    return jnp.concatenate([high, middle, low], axis=0)


def full_dot(wide, weight):
    n = wide.shape[0]
    got = lax.dot_general(three_parts(wide), weight, NT, preferred_element_type=F32)
    return got[:n] + got[n : 2 * n] + got[2 * n :]


def contrast_kernel(pos, got, w_emb, w_out, text_grad, loss, clip_grad, d_out):
    peers = got.shape[0]
    n = 2 * peers
    embedded = jnp.concatenate([got[p, 0:2, :EMB] for p in range(peers)], axis=0)
    weights = jnp.concatenate([got[p, 0:2, EMB:] for p in range(peers)], axis=0)[:, :n]
    words = jnp.concatenate([got[p, 2:4, :EMB] for p in range(peers)], axis=0)
    clip_norm = jnp.sqrt(jnp.sum(embedded * embedded, axis=-1, keepdims=True) + EMBED_EPS)
    text_norm = jnp.sqrt(jnp.sum(words * words, axis=-1, keepdims=True) + EMBED_EPS)
    clip_unit = embedded / clip_norm
    text_unit = words / text_norm
    exact = lax.Precision.HIGHEST
    logits = (
        lax.dot_general(clip_unit, text_unit, NT, precision=exact, preferred_element_type=F32)
        / SOFTMAX_TEMP
    )
    own = lax.broadcasted_iota(jnp.int32, (n, n), 0) == lax.broadcasted_iota(
        jnp.int32, (n, n), 1
    )
    exp_logit = jnp.exp(logits)
    other = jnp.where(own, 0.0, weights)
    negative = other * exp_logit
    diagonal = jnp.where(own, logits, 0.0)
    row_self = jnp.sum(diagonal, axis=1, keepdims=True)
    col_self = jnp.sum(diagonal, axis=0, keepdims=True)
    row_weight = jnp.sum(other, axis=1, keepdims=True)
    col_weight = jnp.sum(other, axis=0, keepdims=True)
    row_part = (
        jnp.exp(row_self) + (n - 1) * jnp.sum(negative, axis=1, keepdims=True) / row_weight
    )
    col_part = (
        jnp.exp(col_self) + (n - 1) * jnp.sum(negative, axis=0, keepdims=True) / col_weight
    )
    summed = jnp.sum(jnp.log(row_part) - row_self, axis=0, keepdims=True) + jnp.sum(
        jnp.log(col_part) - col_self, axis=1, keepdims=True
    )
    loss[...] = summed / (2 * n)
    scaled = (n - 1) * weights * exp_logit
    off = scaled * (1.0 / (row_weight * row_part)) + scaled * (1.0 / (col_weight * col_part))
    on = exp_logit / row_part - 1.0 + exp_logit / col_part - 1.0
    grad = jnp.where(own, on, off)
    d_clip = (
        jnp.dot(grad, text_unit, precision=exact, preferred_element_type=F32) / SOFTMAX_TEMP
    )
    d_text = (
        lax.dot_general(grad, clip_unit, TN, precision=exact, preferred_element_type=F32)
        / SOFTMAX_TEMP
    )
    text_all = (
        d_text - text_unit * jnp.sum(text_unit * d_text, axis=-1, keepdims=True)
    ) / text_norm
    embed_all = (
        d_clip - clip_unit * jnp.sum(clip_unit * d_clip, axis=-1, keepdims=True)
    ) / clip_norm
    row = lax.broadcasted_iota(jnp.int32, (n, 1), 0)

    def mine(array):
        return jnp.concatenate(
            [
                jnp.sum(
                    jnp.where(row == 2 * pos[2] + c, array, 0.0), axis=0, keepdims=True
                )
                for c in range(2)
            ],
            axis=0,
        )

    text_grad[...] = mine(text_all)
    pooled_grad = full_dot(mine(embed_all), w_emb[...])
    clip_grad[...] = pooled_grad
    d_out[...] = full_dot(pooled_grad, w_out[...])


def contrast(pos, got, w_emb, w_out):
    return pl.pallas_call(
        contrast_kernel,
        out_shape=[
            jax.ShapeDtypeStruct((2, EMB), F32),
            jax.ShapeDtypeStruct((1, 1), F32),
            jax.ShapeDtypeStruct((2, D), F32),
            jax.ShapeDtypeStruct((2, D), F32),
        ],
        in_specs=[smem(), vmem(), vmem(), vmem()],
        out_specs=[vmem()] * 4,
        compiler_params=params(),
        name="contrast",
    )(pos, got, w_emb, w_out)


def backward_kernel(clips, shifts, hscale, clip_grad, d_out, *refs):
    nc = len(clips)
    ql, kl, vl, rq, rk, mass, prob, n32, istd, wq, wk, wv = refs[:12]
    outs = refs[12 : 12 + 4 * nc]
    ext, total, ones4, dqs, dks, dqb, dkb, dvb = refs[12 + 4 * nc :]
    step = pl.program_id(0)

    @pl.when(step == 0)
    def _():
        ones4[...] = head_blocks((QW, QW), HEAD_DIM)

    low = low_lanes((TOK, 128))
    upper = lax.broadcasted_iota(jnp.int32, (128, TOK), 0) < HEAD_DIM
    lane = lax.broadcasted_iota(jnp.int32, (1, 128), 1)
    for p in range(2):
        head = step * 4 + 2 * p
        lanes = slice(p * 128, (p + 1) * 128)
        factor = jnp.where(lane < HEAD_DIM, hscale[head], hscale[head + 1])
        for n, c in enumerate(clips):
            row = d_out[c : c + 1, lanes].astype(BF16).astype(F32)
            spread = jnp.transpose(jnp.broadcast_to(row, (TOK, 128)))
            spread = jnp.concatenate(
                [jnp.where(upper, spread, 0.0), jnp.where(upper, 0.0, spread)], axis=1
            ).astype(BF16)
            for w in range(2 * n, 2 * n + 2):
                at = slice(w * TOK, (w + 1) * TOK)
                along = jnp.dot(vl[at, lanes], spread, preferred_element_type=F32)
                pt = prob[0, 2 * w + p]
                inner = jnp.sum(pt * along, axis=0, keepdims=True)
                ds = (pt * (along - inner)).astype(BF16)
                dk = jnp.dot(ds, split_heads(ql[at, lanes]), preferred_element_type=F32)
                dq = lax.dot_general(ds, kl[at, lanes], TN, preferred_element_type=F32)
                dks[at, lanes] = dk * factor
                dqs[at, lanes] = jnp.where(low, dq[:TOK], dq[TOK:]) * factor
                dvb[at, lanes] = (mass[at, lanes] * row).astype(BF16)
    for unit, grad, inverse, done in ((ql, dqs, rq, dqb), (kl, dks, rk, dkb)):
        for w in range(2 * nc):
            at = slice(w * TOK, (w + 1) * TOK)
            u = unit[at].astype(F32)
            g = grad[at]
            inner = jnp.dot((u * g).astype(BF16), ones4[...], preferred_element_type=F32)
            done[at] = ((g - u * inner) * inverse[at]).astype(BF16)
    part = (
        lax.dot_general(dqb[...], wq[...], NT, preferred_element_type=F32)
        + lax.dot_general(dkb[...], wk[...], NT, preferred_element_type=F32)
        + lax.dot_general(dvb[...], wv[...], NT, preferred_element_type=F32)
    )

    @pl.when(step == 0)
    def _():
        total[...] = part

    @pl.when(step > 0)
    def _():
        total[...] = total[...] + part

    @pl.when(step == QUADS - 1)
    def _():
        for n, c in enumerate(clips):
            s0, s1, s2 = shifts[c, 0], shifts[c, 1], shifts[c, 2]
            off0, off1 = s0 + HALO * c, s1 + HALO * c
            turn = (COLS + s2) % COLS
            base = clip_grad[c : c + 1]

            def cells(a, carry):
                for b in range(WH):
                    halves = []
                    for w in range(2):
                        start = pl.multiple_of(
                            (2 * n + w) * TOK + a * (WH * WW) + b * WW, WW
                        )
                        dn = total[pl.ds(start, WW)]
                        y = n32[pl.ds(start, WW)]
                        inv = istd[pl.ds(start, WW)][:, :1]
                        first = jnp.mean(dn, axis=-1, keepdims=True)
                        second = jnp.mean(dn * y, axis=-1, keepdims=True)
                        halves.append(base + inv * (dn - first - y * second))
                    cell = pltpu.roll(jnp.concatenate(halves, axis=0), turn, 0)
                    ext[n, a + off0, b + off1] = cell.astype(BF16)
                return carry

            lax.fori_loop(0, WT, cells, 0)
            f, nf, r, nr = OWN[c]
            outs[4 * n][...] = ext[n, f : f + nf, r : r + nr]
            for k in range(3):
                f, nf, r, nr = PIECES[c][k]
                outs[4 * n + 1 + k][...] = ext[n, f : f + nf, r : r + nr]


def backward(clips, shifts, hscale, clip_grad, d_out, stored, w_qkv):
    nc = len(clips)
    n = nc * 2 * TOK
    column = lambda part: pl.BlockSpec((D, QW), lambda i: (0, part * QUADS + i))
    by_quad = lambda: pl.BlockSpec((n, QW), lambda i: (0, i))
    shapes = ((WT, WH, COLS, D),) + PIECE_SHAPES
    return pl.pallas_call(
        partial(backward_kernel, clips),
        grid=(QUADS,),
        out_shape=[jax.ShapeDtypeStruct(s, BF16) for s in shapes * nc],
        in_specs=[smem(), smem(), whole((2, D)), pl.BlockSpec((2, QW), lambda i: (0, i))]
        + [by_quad() for _ in range(6)]
        + [
            pl.BlockSpec((1, 4 * nc, TOK, 2 * TOK), lambda i: (i, 0, 0, 0)),
            whole((n, D)),
            whole((n, 128)),
            column(0),
            column(1),
            column(2),
        ],
        out_specs=[whole(s) for s in shapes * nc],
        scratch_shapes=[
            pltpu.VMEM((nc, GRID, GRID, COLS, D), BF16),
            pltpu.VMEM((n, D), F32),
            pltpu.VMEM((QW, QW), BF16),
            pltpu.VMEM((n, QW), F32),
            pltpu.VMEM((n, QW), F32),
            pltpu.VMEM((n, QW), BF16),
            pltpu.VMEM((n, QW), BF16),
            pltpu.VMEM((n, QW), BF16),
        ],
        compiler_params=params(dimension_semantics=("arbitrary",)),
        cost_estimate=pl.CostEstimate(
            flops=2 * n * D * 3 * D, bytes_accessed=16 * 2**20, transcendentals=0
        ),
        name="backward",
    )(shifts, hscale, clip_grad, d_out, *stored, w_qkv, w_qkv, w_qkv)


def merge_kernel(shifts, *refs):
    own, got, out = refs[:2], refs[2:8], refs[8]
    for c in range(2):
        s0, s1 = shifts[c, 0], shifts[c, 1]
        a, b, corner = got[3 * c : 3 * c + 3]
        for f in range(WT):
            for r in range(WH):
                if c == 0:
                    far_f, far_r = f < HALO, r < HALO
                    gone_f, gone_r = f < s0, r < s1
                    at_a, at_b, at_c = (f, r - 1), (f - 1, r), (f, r)
                else:
                    far_f, far_r = f >= WT - HALO, r >= WH - HALO
                    gone_f, gone_r = f >= WT + s0, r >= WH + s1
                    at_a, at_b, at_c = (f - 2, r), (f, r - 2), (f - 2, r - 2)
                value = own[c][f, r]
                in_a = far_f and 0 <= at_a[1] < 3
                in_b = far_r and 0 <= at_b[0] < 3
                if in_a:
                    take = jnp.logical_and(gone_f, jnp.logical_not(gone_r))
                    value = jnp.where(take, a[at_a], value)
                if in_b:
                    take = jnp.logical_and(jnp.logical_not(gone_f), gone_r)
                    value = jnp.where(take, b[at_b], value)
                if far_f and far_r:
                    value = jnp.where(jnp.logical_and(gone_f, gone_r), corner[at_c], value)
                out[c, f, r] = value


def merge(shifts, own, got):
    return pl.pallas_call(
        merge_kernel,
        out_shape=jax.ShapeDtypeStruct((2, WT, WH, COLS, D), BF16),
        in_specs=[smem()] + [vmem()] * 8,
        out_specs=vmem(),
        compiler_params=params(),
        name="merge",
    )(shifts, *own, *got)


def local(video, shifts, head_scale, w_qkv, w_out, w_emb, text, bucket, bucket_scale):
    tokens = lax.axis_size("tm") * lax.axis_size("space") * WT * WH * COLS
    plane = lax.axis_size("tm") * lax.axis_size("space")
    peers = lax.axis_size("batch")
    pos = jnp.stack(
        [lax.axis_index("tm"), lax.axis_index("space"), lax.axis_index("batch")]
    ).astype(jnp.int32)
    pieces = pack(video)
    halo = exchange(pieces[:3], 0, -1) + exchange(pieces[3:], 1, -1)
    *stored, sums = forward((0, 1), pos, shifts, head_scale, video, halo, w_qkv)
    spread = jnp.broadcast_to(sums[None], (plane,) + sums.shape)
    got = lax.all_to_all(spread, ("tm", "space"), 0, 0)
    packed = embed(got, w_out, w_emb, text, bucket, bucket_scale, tokens, peers)
    got = lax.all_to_all(packed, "batch", 0, 0)
    text_grad, loss, clip_grad, d_out = contrast(pos, got, w_emb, w_out)
    outs = backward((0, 1), shifts, head_scale, clip_grad, d_out, stored, w_qkv)
    back = exchange(outs[1:4], 0, 1) + exchange(outs[5:8], 1, 1)
    video_grad = merge(shifts, (outs[0], outs[4]), back)
    return (video_grad, text_grad, loss[0, 0])


def solution(mesh):
    in_specs = (
        P("batch", "tm", "space", None, None),
        P("batch", None),
        P(),
        P(),
        P(),
        P(),
        P("batch", None),
        P("batch", None),
        P(),
    )
    out_specs = (P("batch", "tm", "space", None, None), P("batch", None), P())
    return jax.shard_map(local, mesh=mesh, in_specs=in_specs, out_specs=out_specs, check_vma=False)
```

```python
from functools import partial

import jax
import jax.numpy as jnp
from jax import lax
from jax.experimental import pallas as pl
from jax.experimental.pallas import tpu as pltpu
from jax.sharding import PartitionSpec as P

HEADS = 16
HEAD_DIM = 64
D = 1024
EMB = 768
WT = 4
WH = 4
WW = 8
COLS = 16
HALO = 2
TOK = WT * WH * WW
QUADS = 4
QW = 256

SOFTMAX_TEMP = 0.07
NORM_EPS = 1e-05
QUERY_EPS = 1e-06
EMBED_EPS = 1e-06
LOG2E = 1.4426950408889634
F32 = jnp.float32
BF16 = jnp.bfloat16
VMEM_LIMIT = 24 * 1024 * 1024

NT = (((1,), (1,)), ((), ()))
TN = (((0,), (0,)), ((), ()))

GRID = 6
OWN = ((0, 4, 0, 4), (2, 4, 2, 4))
PIECES = (
    ((4, 2, 1, 3), (1, 3, 4, 2), (4, 2, 4, 2)),
    ((0, 2, 2, 3), (2, 3, 0, 2), (0, 2, 0, 2)),
)
GIVEN = (
    ((0, 2, 1, 3), (1, 3, 0, 2), (0, 2, 0, 2)),
    ((2, 2, 0, 3), (0, 3, 2, 2), (2, 2, 2, 2)),
)
PIECE_SHAPES = tuple((g[1], g[3], COLS, D) for g in GIVEN[0])


def vmem():
    return pl.BlockSpec(memory_space=pltpu.VMEM)


def smem():
    return pl.BlockSpec(memory_space=pltpu.SMEM)


def params(**more):
    return pltpu.CompilerParams(vmem_limit_bytes=VMEM_LIMIT, **more)


def pack_kernel(video, *outs):
    for c in range(2):
        for k in range(3):
            f, nf, r, nr = GIVEN[c][k]
            outs[3 * c + k][...] = video[c, f : f + nf, r : r + nr]


def pack(video):
    return pl.pallas_call(
        pack_kernel,
        out_shape=[jax.ShapeDtypeStruct(s, BF16) for s in PIECE_SHAPES * 2],
        in_specs=[vmem()],
        out_specs=[vmem()] * 6,
        compiler_params=params(),
        name="pack",
    )(video)


def exchange(pieces, clip, sign):
    tm, space = lax.axis_size("tm"), lax.axis_size("space")
    step = sign if clip == 0 else -sign
    out = []
    for piece, (dt, ds) in zip(pieces, ((step, 0), (0, step), (step, step))):
        pairs = [
            (t * space + s, ((t + dt) % tm) * space + (s + ds) % space)
            for t in range(tm)
            for s in range(space)
        ]
        out.append(lax.ppermute(piece, ("tm", "space"), pairs))
    return out


def head_blocks(shape, width):
    row = lax.broadcasted_iota(jnp.int32, shape, 0) // width
    lane = lax.broadcasted_iota(jnp.int32, shape, 1) // HEAD_DIM
    return (row == lane).astype(F32).astype(BF16)


def low_lanes(shape):
    return lax.broadcasted_iota(jnp.int32, shape, 1) < HEAD_DIM


def split_heads(pair):
    low = low_lanes((1, 2 * HEAD_DIM)).astype(F32)
    return jnp.concatenate(
        [pair * low.astype(BF16), pair * (1.0 - low).astype(BF16)], axis=0
    )


def window_mask(frame0, row0, col0, s0, s1, s2, frames, rows):
    shape = (TOK, 2 * TOK)

    def label(index):
        f = frame0 + index // (WH * WW) + s0
        r = row0 + (index // WW) % WH + s1
        c = col0 + index % WW + s2
        one = lambda v, n: jnp.where((v < 0) | (v >= n), 1, 0)
        return one(f, frames) * 4 + one(r, rows) * 2 + one(c, COLS)

    key = lax.broadcasted_iota(jnp.int32, shape, 0)
    query = lax.broadcasted_iota(jnp.int32, shape, 1) % TOK
    return jnp.where(label(key) == label(query), 1.0, 0.0)


def forward_kernel(clips, frames, rows_all, pos, shifts, hscale, video, *refs):
    nc = len(clips)
    halo = refs[: 3 * nc]
    w_qkv = refs[3 * nc]
    ql, kl, vl, rq, rk, mass, prob, n32, istd, sums = refs[3 * nc + 1 : 3 * nc + 11]
    ext, xb, masks, ones4, ones2, qs, ks = refs[3 * nc + 11 :]
    ones4[...] = head_blocks((QW, QW), HEAD_DIM)
    ones2[...] = head_blocks((2 * TOK, 2 * HEAD_DIM), TOK)
    for n, c in enumerate(clips):
        f, nf, r, nr = OWN[c]
        ext[n, f : f + nf, r : r + nr] = video[c]
        for k in range(3):
            f, nf, r, nr = PIECES[c][k]
            ext[n, f : f + nf, r : r + nr] = halo[3 * n + k][...]
        s0, s1, s2 = shifts[c, 0], shifts[c, 1], shifts[c, 2]
        off0, off1 = s0 + HALO * c, s1 + HALO * c
        turn = (COLS - s2) % COLS

        def cells(half, total):
            for j in range(2 * WH):
                a, b = 2 * half + j // WH, j % WH
                x = ext[n, a + off0, b + off1].astype(F32)
                total = total + x
                x = pltpu.roll(x, turn, 0)
                centered = x - jnp.mean(x, axis=-1, keepdims=True)
                inv = lax.rsqrt(
                    jnp.mean(centered * centered, axis=-1, keepdims=True) + NORM_EPS
                )
                y = centered * inv
                wide = jnp.broadcast_to(inv, (COLS, 128))
                for w in range(2):
                    start = pl.multiple_of((2 * n + w) * TOK + a * (WH * WW) + b * WW, WW)
                    n32[pl.ds(start, WW)] = y[w * WW : (w + 1) * WW]
                    istd[pl.ds(start, WW)] = wide[w * WW : (w + 1) * WW]
            return total

        total = lax.fori_loop(0, WT // 2, cells, jnp.zeros((COLS, D), F32))
        sums[2 * n : 2 * n + 1] = jnp.sum(total, axis=0, keepdims=True)
        for w in range(2):
            masks[2 * n + w] = window_mask(
                pos[0] * WT, pos[1] * WH, w * WW, s0, s1, s2, frames, rows_all
            )
    xb[...] = n32[...].astype(BF16)
    lane = lax.broadcasted_iota(jnp.int32, (1, 2 * TOK), 1)

    def project(quad):
        jobs = []
        at_quad = slice(quad * QW, (quad + 1) * QW)
        for part in range(3):

            def job(part=part):
                w = w_qkv[:, part * D + quad * QW : part * D + (quad + 1) * QW]
                value = jnp.dot(xb[...], w, preferred_element_type=F32)
                if part == 2:
                    vl[:, at_quad] = value.astype(BF16)
                else:
                    (qs, ks)[part][...] = value

            jobs.append(job)
        for part in range(2):
            for w in range(2 * nc):

                def job(part=part, w=w):
                    at = slice(w * TOK, (w + 1) * TOK)
                    full, unit, inverse = ((qs, ql, rq), (ks, kl, rk))[part]
                    value = full[at]
                    square = jnp.dot(
                        (value * value).astype(BF16), ones4[...], preferred_element_type=F32
                    )
                    inv = lax.rsqrt(square + QUERY_EPS)
                    inverse[at, at_quad] = inv
                    unit[at, at_quad] = (value * inv).astype(BF16)

                jobs.append(job)
        return jobs

    def attend(quad):
        firsts, seconds = [], []
        for p in range(2):
            head = quad * 4 + 2 * p
            lanes = slice(quad * QW + p * 128, quad * QW + (p + 1) * 128)
            for w in range(2 * nc):
                at = slice(w * TOK, (w + 1) * TOK)
                held = {}

                def first(head=head, lanes=lanes, w=w, at=at, p=p, held=held):
                    factor = jnp.where(lane < TOK, hscale[head], hscale[head + 1]) * LOG2E
                    score = lax.dot_general(
                        kl[at, lanes], split_heads(ql[at, lanes]), NT, preferred_element_type=F32
                    )
                    e = jnp.exp2(score * factor) * masks[w]
                    held["e"] = e
                    held["inv"] = 1.0 / jnp.sum(e, axis=0, keepdims=True)

                def second(lanes=lanes, w=w, at=at, p=p, held=held):
                    pt = held["e"] * held["inv"]
                    prob[quad, 2 * w + p] = pt
                    mass_here = jnp.dot(pt.astype(BF16), ones2[...], preferred_element_type=F32)
                    mass[at, lanes] = mass_here
                    gathered = jnp.sum(
                        mass_here * vl[at, lanes].astype(F32), axis=0, keepdims=True
                    )
                    row = slice(w // 2 * 2 + 1, w // 2 * 2 + 2)
                    if w % 2:
                        sums[row, lanes] = sums[row, lanes] + gathered
                    else:
                        sums[row, lanes] = gathered

                firsts.append(first)
                seconds.append(second)
        return staged(firsts, seconds)

    interleave(project(0))
    for quad in range(QUADS):
        interleave(attend(quad), project(quad + 1) if quad + 1 < QUADS else [])


def staged(*stages, lag=3):
    count = len(stages[0])
    jobs = []
    for turn in range(count + lag * (len(stages) - 1)):
        for depth, stage in enumerate(stages):
            unit = turn - lag * depth
            if 0 <= unit < count:
                jobs.append(stage[unit])
    return jobs


def interleave(*lists):
    order = []
    for which, jobs in enumerate(lists):
        for k, job in enumerate(jobs):
            order.append(((k + 0.5) / len(jobs), which, k, job))
    for item in sorted(order, key=lambda t: t[:3]):
        item[3]()


def forward(clips, pos, shifts, hscale, video, halo, w_qkv):
    nc = len(clips)
    n = nc * 2 * TOK
    frames = lax.axis_size("tm") * WT
    rows_all = lax.axis_size("space") * WH
    return pl.pallas_call(
        partial(forward_kernel, clips, frames, rows_all),
        out_shape=[jax.ShapeDtypeStruct((n, D), BF16)] * 3
        + [jax.ShapeDtypeStruct((n, D), F32)] * 3
        + [
            jax.ShapeDtypeStruct((QUADS, 4 * nc, TOK, 2 * TOK), F32),
            jax.ShapeDtypeStruct((n, D), F32),
            jax.ShapeDtypeStruct((n, 128), F32),
            jax.ShapeDtypeStruct((2 * nc, D), F32),
        ],
        in_specs=[smem(), smem(), smem()] + [vmem()] * (2 + 3 * nc),
        out_specs=[vmem()] * 10,
        scratch_shapes=[
            pltpu.VMEM((nc, GRID, GRID, COLS, D), BF16),
            pltpu.VMEM((n, D), BF16),
            pltpu.VMEM((2 * nc, TOK, 2 * TOK), F32),
            pltpu.VMEM((QW, QW), BF16),
            pltpu.VMEM((2 * TOK, 2 * HEAD_DIM), BF16),
            pltpu.VMEM((n, QW), F32),
            pltpu.VMEM((n, QW), F32),
        ],
        compiler_params=params(),
        cost_estimate=pl.CostEstimate(
            flops=2 * n * D * 3 * D, bytes_accessed=12 * 2**20, transcendentals=n * 2048
        ),
        name="forward",
    )(pos, shifts, hscale, video, *halo, w_qkv)


def embed_kernel(tokens, got, w_out, w_emb, text, bucket, levels, out):
    total = jnp.sum(got[...], axis=0)
    mean = (jnp.concatenate([total[1:2], total[3:4]], axis=0) / tokens).astype(BF16)
    token_mean = jnp.concatenate([total[0:1], total[2:3]], axis=0) / tokens
    pooled = token_mean + jnp.dot(mean, w_out[...], preferred_element_type=F32)
    embedded = jnp.dot(pooled.astype(BF16), w_emb[...], preferred_element_type=F32)
    held = bucket[...]
    weight = jnp.zeros(held.shape, F32)
    for level in range(levels.shape[0]):
        weight = weight + jnp.where(held == level, levels[level], 0.0)
    weight = jnp.concatenate(
        [weight, jnp.zeros((held.shape[0], 128 - held.shape[1]), F32)], axis=1
    )
    words = text[...].astype(F32)
    block = jnp.concatenate(
        [
            jnp.concatenate([embedded, weight], axis=1),
            jnp.concatenate([words, jnp.zeros_like(weight)], axis=1),
        ],
        axis=0,
    )
    for peer in range(out.shape[0]):
        out[peer] = block


def embed(got, w_out, w_emb, text, bucket, levels, tokens, peers):
    return pl.pallas_call(
        partial(embed_kernel, tokens),
        out_shape=jax.ShapeDtypeStruct((peers, 4, EMB + 128), F32),
        in_specs=[vmem()] * 5 + [smem()],
        out_specs=vmem(),
        compiler_params=params(),
        name="embed",
    )(got, w_out, w_emb, text, bucket, levels)


def three_parts(wide):
    high = wide.astype(BF16)
    rest = wide - high.astype(F32)
    middle = rest.astype(BF16)
    low = (rest - middle.astype(F32)).astype(BF16)
    return jnp.concatenate([high, middle, low], axis=0)


def full_dot(wide, weight):
    n = wide.shape[0]
    got = lax.dot_general(three_parts(wide), weight, NT, preferred_element_type=F32)
    return got[:n] + got[n : 2 * n] + got[2 * n :]


def contrast_kernel(pos, got, w_emb, w_out, text_grad, loss, clip_grad, d_out):
    peers = got.shape[0]
    n = 2 * peers
    embedded = jnp.concatenate([got[p, 0:2, :EMB] for p in range(peers)], axis=0)
    weights = jnp.concatenate([got[p, 0:2, EMB:] for p in range(peers)], axis=0)[:, :n]
    words = jnp.concatenate([got[p, 2:4, :EMB] for p in range(peers)], axis=0)
    clip_norm = jnp.sqrt(jnp.sum(embedded * embedded, axis=-1, keepdims=True) + EMBED_EPS)
    text_norm = jnp.sqrt(jnp.sum(words * words, axis=-1, keepdims=True) + EMBED_EPS)
    clip_unit = embedded / clip_norm
    text_unit = words / text_norm
    exact = lax.Precision.HIGHEST
    logits = (
        lax.dot_general(clip_unit, text_unit, NT, precision=exact, preferred_element_type=F32)
        / SOFTMAX_TEMP
    )
    own = lax.broadcasted_iota(jnp.int32, (n, n), 0) == lax.broadcasted_iota(
        jnp.int32, (n, n), 1
    )
    exp_logit = jnp.exp(logits)
    other = jnp.where(own, 0.0, weights)
    negative = other * exp_logit
    diagonal = jnp.where(own, logits, 0.0)
    row_self = jnp.sum(diagonal, axis=1, keepdims=True)
    col_self = jnp.sum(diagonal, axis=0, keepdims=True)
    row_weight = jnp.sum(other, axis=1, keepdims=True)
    col_weight = jnp.sum(other, axis=0, keepdims=True)
    row_part = (
        jnp.exp(row_self) + (n - 1) * jnp.sum(negative, axis=1, keepdims=True) / row_weight
    )
    col_part = (
        jnp.exp(col_self) + (n - 1) * jnp.sum(negative, axis=0, keepdims=True) / col_weight
    )
    summed = jnp.sum(jnp.log(row_part) - row_self, axis=0, keepdims=True) + jnp.sum(
        jnp.log(col_part) - col_self, axis=1, keepdims=True
    )
    loss[...] = summed / (2 * n)
    scaled = (n - 1) * weights * exp_logit
    off = scaled * (1.0 / (row_weight * row_part)) + scaled * (1.0 / (col_weight * col_part))
    on = exp_logit / row_part - 1.0 + exp_logit / col_part - 1.0
    grad = jnp.where(own, on, off)
    d_clip = (
        jnp.dot(grad, text_unit, precision=exact, preferred_element_type=F32) / SOFTMAX_TEMP
    )
    d_text = (
        lax.dot_general(grad, clip_unit, TN, precision=exact, preferred_element_type=F32)
        / SOFTMAX_TEMP
    )
    text_all = (
        d_text - text_unit * jnp.sum(text_unit * d_text, axis=-1, keepdims=True)
    ) / text_norm
    embed_all = (
        d_clip - clip_unit * jnp.sum(clip_unit * d_clip, axis=-1, keepdims=True)
    ) / clip_norm
    row = lax.broadcasted_iota(jnp.int32, (n, 1), 0)

    def mine(array):
        return jnp.concatenate(
            [
                jnp.sum(
                    jnp.where(row == 2 * pos[2] + c, array, 0.0), axis=0, keepdims=True
                )
                for c in range(2)
            ],
            axis=0,
        )

    text_grad[...] = mine(text_all)
    pooled_grad = full_dot(mine(embed_all), w_emb[...])
    clip_grad[...] = pooled_grad
    d_out[...] = full_dot(pooled_grad, w_out[...])


def contrast(pos, got, w_emb, w_out):
    return pl.pallas_call(
        contrast_kernel,
        out_shape=[
            jax.ShapeDtypeStruct((2, EMB), F32),
            jax.ShapeDtypeStruct((1, 1), F32),
            jax.ShapeDtypeStruct((2, D), F32),
            jax.ShapeDtypeStruct((2, D), F32),
        ],
        in_specs=[smem(), vmem(), vmem(), vmem()],
        out_specs=[vmem()] * 4,
        compiler_params=params(),
        name="contrast",
    )(pos, got, w_emb, w_out)


def backward_kernel(clips, shifts, hscale, clip_grad, d_out, *refs):
    nc = len(clips)
    ql, kl, vl, rq, rk, mass, prob, n32, istd, w_qkv = refs[:10]
    outs = refs[10 : 10 + 4 * nc]
    ext, total, ones4, dqs, dks, dqb, dkb, dvb = refs[10 + 4 * nc :]
    rows = nc * 2 * TOK
    ones4[...] = head_blocks((QW, QW), HEAD_DIM)
    low = low_lanes((TOK, 128))
    upper = lax.broadcasted_iota(jnp.int32, (128, TOK), 0) < HEAD_DIM
    lane = lax.broadcasted_iota(jnp.int32, (1, 128), 1)

    def attend(quad):
        firsts, seconds, thirds, norms = [], [], [], []
        for n, c in enumerate(clips):
            for p in range(2):
                head = quad * 4 + 2 * p
                lanes = slice(quad * QW + p * 128, quad * QW + (p + 1) * 128)
                factor = jnp.where(lane < HEAD_DIM, hscale[head], hscale[head + 1])
                shared = {}
                for w in range(2 * n, 2 * n + 2):
                    at = slice(w * TOK, (w + 1) * TOK)
                    held = {}

                    def first(lanes=lanes, w=w, p=p, c=c, at=at, shared=shared, held=held):
                        if not shared:
                            row = d_out[c : c + 1, lanes].astype(BF16).astype(F32)
                            spread = jnp.transpose(jnp.broadcast_to(row, (TOK, 128)))
                            shared["row"] = row
                            shared["spread"] = jnp.concatenate(
                                [jnp.where(upper, spread, 0.0), jnp.where(upper, 0.0, spread)],
                                axis=1,
                            ).astype(BF16)
                        along = jnp.dot(
                            vl[at, lanes], shared["spread"], preferred_element_type=F32
                        )
                        pt = prob[quad, 2 * w + p]
                        inner = jnp.sum(pt * along, axis=0, keepdims=True)
                        held["ds"] = (pt * (along - inner)).astype(BF16)
                        dvb[at, lanes] = (mass[at, lanes] * shared["row"]).astype(BF16)

                    def second(lanes=lanes, at=at, factor=factor, held=held):
                        ds = held["ds"]
                        dk = jnp.dot(ds, split_heads(ql[at, lanes]), preferred_element_type=F32)
                        dks[at, lanes] = dk * factor
                        held["turned"] = jnp.concatenate(
                            [jnp.transpose(ds[:, :TOK]), jnp.transpose(ds[:, TOK:])], axis=1
                        )

                    def third(lanes=lanes, at=at, factor=factor, held=held):
                        dq = jnp.dot(
                            held["turned"],
                            split_heads(kl[at, lanes]),
                            preferred_element_type=F32,
                        )
                        dqs[at, lanes] = dq * factor

                    firsts.append(first)
                    seconds.append(second)
                    thirds.append(third)
            for w in range(2 * n, 2 * n + 2):
                for part in range(2):

                    def job(w=w, part=part):
                        unit, grad, inverse, done = (
                            (ql, dqs, rq, dqb),
                            (kl, dks, rk, dkb),
                        )[part]
                        at = slice(w * TOK, (w + 1) * TOK)
                        q = slice(quad * QW, (quad + 1) * QW)
                        u = unit[at, q].astype(F32)
                        g = grad[at, q]
                        inner = jnp.dot(
                            (u * g).astype(BF16), ones4[...], preferred_element_type=F32
                        )
                        done[at, q] = ((g - u * inner) * inverse[at, q]).astype(BF16)

                    norms.append(job)
        return staged(firsts, seconds, thirds, lag=2) + norms

    def collect(quad):
        jobs = []
        for part in range(0, D, QW):

            def job(part=part):
                cols = slice(part, part + QW)
                got = None
                for k, grad in enumerate((dqb, dkb, dvb)):
                    term = lax.dot_general(
                        grad[:, quad * QW : (quad + 1) * QW],
                        w_qkv[cols, k * D + quad * QW : k * D + (quad + 1) * QW],
                        NT,
                        preferred_element_type=F32,
                    )
                    got = term if got is None else got + term
                total[:, cols] = got if quad == 0 else total[:, cols] + got

            jobs.append(job)
        return jobs

    for quad in range(QUADS):
        interleave(attend(quad), collect(quad - 1) if quad else [])
    interleave(collect(QUADS - 1))
    for n, c in enumerate(clips):
        s0, s1, s2 = shifts[c, 0], shifts[c, 1], shifts[c, 2]
        off0, off1 = s0 + HALO * c, s1 + HALO * c
        turn = (COLS + s2) % COLS
        base = clip_grad[c : c + 1]

        def cells(half, carry):
            for j in range(2 * WH):
                a, b = 2 * half + j // WH, j % WH
                halves = []
                for w in range(2):
                    start = pl.multiple_of((2 * n + w) * TOK + a * (WH * WW) + b * WW, WW)
                    dn = total[pl.ds(start, WW)]
                    y = n32[pl.ds(start, WW)]
                    inv = istd[pl.ds(start, WW)][:, :1]
                    first = jnp.mean(dn, axis=-1, keepdims=True)
                    second = jnp.mean(dn * y, axis=-1, keepdims=True)
                    halves.append(base + inv * (dn - first - y * second))
                cell = pltpu.roll(jnp.concatenate(halves, axis=0), turn, 0)
                ext[n, a + off0, b + off1] = cell.astype(BF16)
            return carry

        lax.fori_loop(0, WT // 2, cells, 0)
        f, nf, r, nr = OWN[c]
        outs[4 * n][...] = ext[n, f : f + nf, r : r + nr]
        for k in range(3):
            f, nf, r, nr = PIECES[c][k]
            outs[4 * n + 1 + k][...] = ext[n, f : f + nf, r : r + nr]


def backward(clips, shifts, hscale, clip_grad, d_out, stored, w_qkv):
    nc = len(clips)
    n = nc * 2 * TOK
    shapes = ((WT, WH, COLS, D),) + PIECE_SHAPES
    return pl.pallas_call(
        partial(backward_kernel, clips),
        out_shape=[jax.ShapeDtypeStruct(s, BF16) for s in shapes * nc],
        in_specs=[smem(), smem()] + [vmem()] * 12,
        out_specs=[vmem()] * (4 * nc),
        scratch_shapes=[
            pltpu.VMEM((nc, GRID, GRID, COLS, D), BF16),
            pltpu.VMEM((n, D), F32),
            pltpu.VMEM((QW, QW), BF16),
            pltpu.VMEM((n, D), F32),
            pltpu.VMEM((n, D), F32),
            pltpu.VMEM((n, D), BF16),
            pltpu.VMEM((n, D), BF16),
            pltpu.VMEM((n, D), BF16),
        ],
        compiler_params=params(),
        cost_estimate=pl.CostEstimate(
            flops=2 * n * D * 3 * D, bytes_accessed=16 * 2**20, transcendentals=0
        ),
        name="backward",
    )(shifts, hscale, clip_grad, d_out, *stored, w_qkv)


def merge_kernel(shifts, *refs):
    own, got, out = refs[:2], refs[2:8], refs[8]
    for c in range(2):
        s0, s1 = shifts[c, 0], shifts[c, 1]
        a, b, corner = got[3 * c : 3 * c + 3]
        for f in range(WT):
            for r in range(WH):
                if c == 0:
                    far_f, far_r = f < HALO, r < HALO
                    gone_f, gone_r = f < s0, r < s1
                    at_a, at_b, at_c = (f, r - 1), (f - 1, r), (f, r)
                else:
                    far_f, far_r = f >= WT - HALO, r >= WH - HALO
                    gone_f, gone_r = f >= WT + s0, r >= WH + s1
                    at_a, at_b, at_c = (f - 2, r), (f, r - 2), (f - 2, r - 2)
                value = own[c][f, r]
                in_a = far_f and 0 <= at_a[1] < 3
                in_b = far_r and 0 <= at_b[0] < 3
                if in_a:
                    take = jnp.logical_and(gone_f, jnp.logical_not(gone_r))
                    value = jnp.where(take, a[at_a], value)
                if in_b:
                    take = jnp.logical_and(jnp.logical_not(gone_f), gone_r)
                    value = jnp.where(take, b[at_b], value)
                if far_f and far_r:
                    value = jnp.where(jnp.logical_and(gone_f, gone_r), corner[at_c], value)
                out[c, f, r] = value


def merge(shifts, own, got):
    return pl.pallas_call(
        merge_kernel,
        out_shape=jax.ShapeDtypeStruct((2, WT, WH, COLS, D), BF16),
        in_specs=[smem()] + [vmem()] * 8,
        out_specs=vmem(),
        compiler_params=params(),
        name="merge",
    )(shifts, *own, *got)


def local(video, shifts, head_scale, w_qkv, w_out, w_emb, text, bucket, bucket_scale):
    tokens = lax.axis_size("tm") * lax.axis_size("space") * WT * WH * COLS
    plane = lax.axis_size("tm") * lax.axis_size("space")
    peers = lax.axis_size("batch")
    pos = jnp.stack(
        [lax.axis_index("tm"), lax.axis_index("space"), lax.axis_index("batch")]
    ).astype(jnp.int32)
    pieces = pack(video)
    halo = exchange(pieces[:3], 0, -1) + exchange(pieces[3:], 1, -1)
    *stored, sums = forward((0, 1), pos, shifts, head_scale, video, halo, w_qkv)
    spread = jnp.broadcast_to(sums[None], (plane,) + sums.shape)
    got = lax.all_to_all(spread, ("tm", "space"), 0, 0)
    packed = embed(got, w_out, w_emb, text, bucket, bucket_scale, tokens, peers)
    got = lax.all_to_all(packed, "batch", 0, 0)
    text_grad, loss, clip_grad, d_out = contrast(pos, got, w_emb, w_out)
    outs = backward((0, 1), shifts, head_scale, clip_grad, d_out, stored, w_qkv)
    back = exchange(outs[1:4], 0, 1) + exchange(outs[5:8], 1, 1)
    video_grad = merge(shifts, (outs[0], outs[4]), back)
    return (video_grad, text_grad, loss[0, 0])


def solution(mesh):
    in_specs = (
        P("batch", "tm", "space", None, None),
        P("batch", None),
        P(),
        P(),
        P(),
        P(),
        P("batch", None),
        P("batch", None),
        P(),
    )
    out_specs = (P("batch", "tm", "space", None, None), P("batch", None), P())
    return jax.shard_map(local, mesh=mesh, in_specs=in_specs, out_specs=out_specs, check_vma=False)
```

```python
from functools import partial

import jax
import jax.numpy as jnp
from jax import lax
from jax.experimental import pallas as pl
from jax.experimental.pallas import tpu as pltpu
from jax.sharding import PartitionSpec as P

HEADS = 16
HEAD_DIM = 64
D = 1024
EMB = 768
WT = 4
WH = 4
WW = 8
COLS = 16
HALO = 2
TOK = WT * WH * WW
QUADS = 4
QW = 256

SOFTMAX_TEMP = 0.07
NORM_EPS = 1e-05
QUERY_EPS = 1e-06
EMBED_EPS = 1e-06
LOG2E = 1.4426950408889634
F32 = jnp.float32
BF16 = jnp.bfloat16
MIB = 1024 * 1024

NN = (((1,), (0,)), ((), ()))
NT = (((1,), (1,)), ((), ()))
TN = (((0,), (0,)), ((), ()))

GRID = 6
OWN = ((0, 4, 0, 4), (2, 4, 2, 4))
PIECES = (
    ((4, 2, 1, 3), (1, 3, 4, 2), (4, 2, 4, 2)),
    ((0, 2, 2, 3), (2, 3, 0, 2), (0, 2, 0, 2)),
)
GIVEN = (
    ((0, 2, 1, 3), (1, 3, 0, 2), (0, 2, 0, 2)),
    ((2, 2, 0, 3), (0, 3, 2, 2), (2, 2, 2, 2)),
)
PIECE_SHAPES = tuple((g[1], g[3], COLS, D) for g in GIVEN[0])


def vmem():
    return pl.BlockSpec(memory_space=pltpu.VMEM)


def smem():
    return pl.BlockSpec(memory_space=pltpu.SMEM)


def params(mib):
    return pltpu.CompilerParams(vmem_limit_bytes=mib * MIB)


def pack_kernel(video, *outs):
    for c in range(2):
        for k in range(3):
            f, nf, r, nr = GIVEN[c][k]
            outs[3 * c + k][...] = video[c, f : f + nf, r : r + nr]


def pack(video):
    return pl.pallas_call(
        pack_kernel,
        out_shape=[jax.ShapeDtypeStruct(s, BF16) for s in PIECE_SHAPES * 2],
        in_specs=[vmem()],
        out_specs=[vmem()] * 6,
        compiler_params=params(4),
        name="pack",
    )(video)


def load_kernel(after, w_hbm, video_hbm, shifts, hscale, w_out, video_out, shifts_out, scale_out, sems):
    copies = [
        pltpu.make_async_copy(w_hbm, w_out, sems.at[0]),
        pltpu.make_async_copy(video_hbm, video_out, sems.at[1]),
    ]
    for copy in copies:
        copy.start()
    for c in range(2):
        for k in range(3):
            shifts_out[c, k] = shifts[c, k]
    for h in range(HEADS):
        scale_out[h] = hscale[h]
    for copy in copies:
        copy.wait()


def load(after, w_qkv, video, shifts, hscale):
    return pl.pallas_call(
        load_kernel,
        out_shape=[
            jax.ShapeDtypeStruct(x.shape, x.dtype) for x in (w_qkv, video, shifts, hscale)
        ],
        in_specs=[pl.BlockSpec(memory_space=pl.ANY)] * 3 + [smem()] * 2,
        out_specs=[vmem()] * 2 + [smem()] * 2,
        scratch_shapes=[pltpu.SemaphoreType.DMA((2,))],
        compiler_params=params(4),
        cost_estimate=pl.CostEstimate(
            flops=0, bytes_accessed=2 * (w_qkv.size + video.size), transcendentals=0
        ),
        name="load",
    )(after, w_qkv, video, shifts, hscale)


def exchange(pieces, clip, sign):
    tm, space = lax.axis_size("tm"), lax.axis_size("space")
    step = sign if clip == 0 else -sign
    out = []
    for piece, (dt, ds) in zip(pieces, ((step, 0), (0, step), (step, step))):
        pairs = [
            (t * space + s, ((t + dt) % tm) * space + (s + ds) % space)
            for t in range(tm)
            for s in range(space)
        ]
        out.append(lax.ppermute(piece, ("tm", "space"), pairs))
    return out


def head_blocks(shape, width):
    row = lax.broadcasted_iota(jnp.int32, shape, 0) // width
    lane = lax.broadcasted_iota(jnp.int32, shape, 1) // HEAD_DIM
    return (row == lane).astype(F32).astype(BF16)


def low_lanes(shape):
    return lax.broadcasted_iota(jnp.int32, shape, 1) < HEAD_DIM


def split_heads(pair):
    low = low_lanes((1, 2 * HEAD_DIM)).astype(F32)
    return jnp.concatenate(
        [pair * low.astype(BF16), pair * (1.0 - low).astype(BF16)], axis=0
    )


def window_mask(frame0, row0, col0, s0, s1, s2, frames, rows):
    shape = (TOK, 2 * TOK)

    def label(index):
        f = frame0 + index // (WH * WW) + s0
        r = row0 + (index // WW) % WH + s1
        c = col0 + index % WW + s2
        one = lambda v, n: jnp.where((v < 0) | (v >= n), 1, 0)
        return one(f, frames) * 4 + one(r, rows) * 2 + one(c, COLS)

    key = lax.broadcasted_iota(jnp.int32, shape, 0)
    query = lax.broadcasted_iota(jnp.int32, shape, 1) % TOK
    return jnp.where(label(key) == label(query), 1.0, 0.0)


def forward_kernel(clips, frames, rows_all, shifts, hscale, video, *refs):
    nc = len(clips)
    frame0 = lax.axis_index("tm") * WT
    row0 = lax.axis_index("space") * WH
    halo, refs = refs[: 3 * nc], refs[3 * nc :]
    w_qkv, refs = refs[0], refs[1:]
    ql, kl, vl, rq, rk, mass, prob, n32, istd, sums = refs[:10]
    ext, xb, masks, ones4, ones2, qs, ks = refs[10:]
    ones4[...] = head_blocks((QW, QW), HEAD_DIM)
    ones2[...] = head_blocks((2 * TOK, 2 * HEAD_DIM), TOK)
    for n, c in enumerate(clips):
        f, nf, r, nr = OWN[c]
        ext[n, f : f + nf, r : r + nr] = video[c]
        for k in range(3):
            f, nf, r, nr = PIECES[c][k]
            ext[n, f : f + nf, r : r + nr] = halo[3 * n + k][...]
        s0, s1, s2 = shifts[c, 0], shifts[c, 1], shifts[c, 2]
        off0, off1 = s0 + HALO * c, s1 + HALO * c
        turn = (COLS - s2) % COLS

        def cells(half, total):
            for j in range(2 * WH):
                a, b = 2 * half + j // WH, j % WH
                x = ext[n, a + off0, b + off1].astype(F32)
                total = total + x
                x = pltpu.roll(x, turn, 0)
                centered = x - jnp.mean(x, axis=-1, keepdims=True)
                inv = lax.rsqrt(
                    jnp.mean(centered * centered, axis=-1, keepdims=True) + NORM_EPS
                )
                y = centered * inv
                wide = jnp.broadcast_to(inv, (COLS, 128))
                for w in range(2):
                    start = pl.multiple_of((2 * n + w) * TOK + a * (WH * WW) + b * WW, WW)
                    n32[pl.ds(start, WW)] = y[w * WW : (w + 1) * WW]
                    istd[pl.ds(start, WW)] = wide[w * WW : (w + 1) * WW]
            return total

        total = lax.fori_loop(0, WT // 2, cells, jnp.zeros((COLS, D), F32))
        sums[2 * n : 2 * n + 1] = jnp.sum(total, axis=0, keepdims=True)
        for w in range(2):
            masks[2 * n + w] = window_mask(
                frame0, row0, w * WW, s0, s1, s2, frames, rows_all
            )
    xb[...] = n32[...].astype(BF16)
    lane = lax.broadcasted_iota(jnp.int32, (1, 2 * TOK), 1)

    def project(quad):
        jobs = []
        at_quad = slice(quad * QW, (quad + 1) * QW)
        for part in range(3):

            def job(part=part):
                w = w_qkv[:, part * D + quad * QW : part * D + (quad + 1) * QW]
                value = jnp.dot(xb[...], w, preferred_element_type=F32)
                if part == 2:
                    vl[:, at_quad] = value.astype(BF16)
                else:
                    (qs, ks)[part][...] = value

            jobs.append(job)
        for part in range(2):
            for w in range(2 * nc):

                def job(part=part, w=w):
                    at = slice(w * TOK, (w + 1) * TOK)
                    full, unit, inverse = ((qs, ql, rq), (ks, kl, rk))[part]
                    value = full[at]
                    square = jnp.dot(
                        (value * value).astype(BF16), ones4[...], preferred_element_type=F32
                    )
                    inv = lax.rsqrt(square + QUERY_EPS)
                    inverse[at, at_quad] = inv
                    unit[at, at_quad] = (value * inv).astype(BF16)

                jobs.append(job)
        return jobs

    def attend(quad):
        firsts, seconds = [], []
        for p in range(2):
            head = quad * 4 + 2 * p
            lanes = slice(quad * QW + p * 128, quad * QW + (p + 1) * 128)
            for w in range(2 * nc):
                at = slice(w * TOK, (w + 1) * TOK)
                held = {}

                def first(head=head, lanes=lanes, w=w, at=at, p=p, held=held):
                    factor = jnp.where(lane < TOK, hscale[head], hscale[head + 1]) * LOG2E
                    score = lax.dot_general(
                        kl[at, lanes], split_heads(ql[at, lanes]), NT, preferred_element_type=F32
                    )
                    e = jnp.exp2(score * factor) * masks[w]
                    held["e"] = e
                    held["inv"] = 1.0 / jnp.sum(e, axis=0, keepdims=True)

                def second(lanes=lanes, w=w, at=at, p=p, held=held):
                    pt = held["e"] * held["inv"]
                    prob[quad, 2 * w + p] = pt
                    mass_here = jnp.dot(pt.astype(BF16), ones2[...], preferred_element_type=F32)
                    mass[at, lanes] = mass_here
                    gathered = jnp.sum(
                        mass_here * vl[at, lanes].astype(F32), axis=0, keepdims=True
                    )
                    row = slice(w // 2 * 2 + 1, w // 2 * 2 + 2)
                    if w % 2:
                        sums[row, lanes] = sums[row, lanes] + gathered
                    else:
                        sums[row, lanes] = gathered

                firsts.append(first)
                seconds.append(second)
        return staged(firsts, seconds)

    interleave(project(0))
    for quad in range(QUADS):
        interleave(attend(quad), project(quad + 1) if quad + 1 < QUADS else [])


def staged(*stages, lag=3):
    count = len(stages[0])
    jobs = []
    for turn in range(count + lag * (len(stages) - 1)):
        for depth, stage in enumerate(stages):
            unit = turn - lag * depth
            if 0 <= unit < count:
                jobs.append(stage[unit])
    return jobs


def interleave(*lists):
    order = []
    for which, jobs in enumerate(lists):
        for k, job in enumerate(jobs):
            order.append(((k + 0.5) / len(jobs), which, k, job))
    for item in sorted(order, key=lambda t: t[:3]):
        item[3]()


def forward(shifts, hscale, video, halo, w_qkv):
    clips = (0, 1)
    nc = len(clips)
    n = nc * 2 * TOK
    frames = lax.axis_size("tm") * WT
    rows_all = lax.axis_size("space") * WH
    return pl.pallas_call(
        partial(forward_kernel, clips, frames, rows_all),
        out_shape=[jax.ShapeDtypeStruct((n, D), BF16)] * 3
        + [jax.ShapeDtypeStruct((n, D), F32)] * 3
        + [
            jax.ShapeDtypeStruct((QUADS, 4 * nc, TOK, 2 * TOK), F32),
            jax.ShapeDtypeStruct((n, D), F32),
            jax.ShapeDtypeStruct((n, 128), F32),
            jax.ShapeDtypeStruct((2 * nc, D), F32),
        ],
        in_specs=[smem(), smem()] + [vmem()] * (2 + 3 * nc),
        out_specs=[vmem()] * 10,
        scratch_shapes=[
            pltpu.VMEM((nc, GRID, GRID, COLS, D), BF16),
            pltpu.VMEM((n, D), BF16),
            pltpu.VMEM((2 * nc, TOK, 2 * TOK), F32),
            pltpu.VMEM((QW, QW), BF16),
            pltpu.VMEM((2 * TOK, 2 * HEAD_DIM), BF16),
            pltpu.VMEM((n, QW), F32),
            pltpu.VMEM((n, QW), F32),
        ],
        compiler_params=params(12),
        cost_estimate=pl.CostEstimate(
            flops=2 * n * D * 3 * D, bytes_accessed=12 * 2**20, transcendentals=n * 2048
        ),
        name="forward",
    )(shifts, hscale, video, *halo, w_qkv)


def share_kernel(tokens, sums, w_out, w_emb, out):
    means = sums[...] / tokens
    pooled = jnp.concatenate([means[0:1], means[2:3]], axis=0) + full_dot(
        jnp.concatenate([means[1:2], means[3:4]], axis=0), w_out[...], NN
    )
    block = full_dot(pooled, w_emb[...], NN)
    for peer in range(out.shape[0]):
        out[peer] = block


def share(sums, w_out, w_emb, tokens):
    plane = lax.axis_size("tm") * lax.axis_size("space")
    return pl.pallas_call(
        partial(share_kernel, tokens),
        out_shape=jax.ShapeDtypeStruct((plane, 2, EMB), F32),
        in_specs=[vmem()] * 3,
        out_specs=vmem(),
        compiler_params=params(4),
        name="share",
    )(sums, w_out, w_emb)


def embed_kernel(got, text, bucket, levels, out):
    embedded = jnp.sum(got[...], axis=0)
    held = bucket[...]
    weight = jnp.zeros(held.shape, F32)
    for level in range(levels.shape[0]):
        weight = weight + jnp.where(held == level, levels[level], 0.0)
    weight = jnp.concatenate(
        [weight, jnp.zeros((held.shape[0], 128 - held.shape[1]), F32)], axis=1
    )
    words = text[...].astype(F32)
    block = jnp.concatenate(
        [
            jnp.concatenate([embedded, weight], axis=1),
            jnp.concatenate([words, jnp.zeros_like(weight)], axis=1),
        ],
        axis=0,
    )
    for peer in range(out.shape[0]):
        out[peer] = block


def embed(got, text, bucket, levels, peers):
    return pl.pallas_call(
        embed_kernel,
        out_shape=jax.ShapeDtypeStruct((peers, 4, EMB + 128), F32),
        in_specs=[vmem()] * 3 + [smem()],
        out_specs=vmem(),
        compiler_params=params(4),
        name="embed",
    )(got, text, bucket, levels)


def three_parts(wide):
    high = wide.astype(BF16)
    rest = wide - high.astype(F32)
    middle = rest.astype(BF16)
    low = (rest - middle.astype(F32)).astype(BF16)
    return jnp.concatenate([high, middle, low], axis=0)


def full_dot(wide, weight, dims):
    n = wide.shape[0]
    got = lax.dot_general(three_parts(wide), weight, dims, preferred_element_type=F32)
    return got[:n] + got[n : 2 * n] + got[2 * n :]


def contrast_kernel(got, w_emb, w_out, text_grad, loss, clip_grad, d_out):
    peers = got.shape[0]
    n = 2 * peers
    first_clip = 2 * lax.axis_index("batch")
    embedded = jnp.concatenate([got[p, 0:2, :EMB] for p in range(peers)], axis=0)
    weights = jnp.concatenate([got[p, 0:2, EMB:] for p in range(peers)], axis=0)[:, :n]
    words = jnp.concatenate([got[p, 2:4, :EMB] for p in range(peers)], axis=0)
    clip_norm = jnp.sqrt(jnp.sum(embedded * embedded, axis=-1, keepdims=True) + EMBED_EPS)
    text_norm = jnp.sqrt(jnp.sum(words * words, axis=-1, keepdims=True) + EMBED_EPS)
    clip_unit = embedded / clip_norm
    text_unit = words / text_norm
    exact = lax.Precision.HIGHEST
    logits = (
        lax.dot_general(clip_unit, text_unit, NT, precision=exact, preferred_element_type=F32)
        / SOFTMAX_TEMP
    )
    own = lax.broadcasted_iota(jnp.int32, (n, n), 0) == lax.broadcasted_iota(
        jnp.int32, (n, n), 1
    )
    exp_logit = jnp.exp(logits)
    other = jnp.where(own, 0.0, weights)
    negative = other * exp_logit
    diagonal = jnp.where(own, logits, 0.0)
    row_self = jnp.sum(diagonal, axis=1, keepdims=True)
    col_self = jnp.sum(diagonal, axis=0, keepdims=True)
    row_weight = jnp.sum(other, axis=1, keepdims=True)
    col_weight = jnp.sum(other, axis=0, keepdims=True)
    row_part = (
        jnp.exp(row_self) + (n - 1) * jnp.sum(negative, axis=1, keepdims=True) / row_weight
    )
    col_part = (
        jnp.exp(col_self) + (n - 1) * jnp.sum(negative, axis=0, keepdims=True) / col_weight
    )
    summed = jnp.sum(jnp.log(row_part) - row_self, axis=0, keepdims=True) + jnp.sum(
        jnp.log(col_part) - col_self, axis=1, keepdims=True
    )
    loss[...] = summed / (2 * n)
    scaled = (n - 1) * weights * exp_logit
    off = scaled * (1.0 / (row_weight * row_part)) + scaled * (1.0 / (col_weight * col_part))
    on = exp_logit / row_part - 1.0 + exp_logit / col_part - 1.0
    grad = jnp.where(own, on, off)
    d_clip = (
        jnp.dot(grad, text_unit, precision=exact, preferred_element_type=F32) / SOFTMAX_TEMP
    )
    d_text = (
        lax.dot_general(grad, clip_unit, TN, precision=exact, preferred_element_type=F32)
        / SOFTMAX_TEMP
    )
    text_all = (
        d_text - text_unit * jnp.sum(text_unit * d_text, axis=-1, keepdims=True)
    ) / text_norm
    embed_all = (
        d_clip - clip_unit * jnp.sum(clip_unit * d_clip, axis=-1, keepdims=True)
    ) / clip_norm
    row = lax.broadcasted_iota(jnp.int32, (n, 1), 0)

    def mine(array):
        return jnp.concatenate(
            [
                jnp.sum(
                    jnp.where(row == first_clip + c, array, 0.0), axis=0, keepdims=True
                )
                for c in range(2)
            ],
            axis=0,
        )

    text_grad[...] = mine(text_all)
    pooled_grad = full_dot(mine(embed_all), w_emb[...], NT)
    clip_grad[...] = pooled_grad
    d_out[...] = full_dot(pooled_grad, w_out[...], NT)


def contrast(got, w_emb, w_out):
    return pl.pallas_call(
        contrast_kernel,
        out_shape=[
            jax.ShapeDtypeStruct((2, EMB), F32),
            jax.ShapeDtypeStruct((1, 1), F32),
            jax.ShapeDtypeStruct((2, D), F32),
            jax.ShapeDtypeStruct((2, D), F32),
        ],
        in_specs=[vmem()] * 3,
        out_specs=[vmem()] * 4,
        compiler_params=params(4),
        name="contrast",
    )(got, w_emb, w_out)


def backward_kernel(clips, shifts, hscale, clip_grad, d_out, *refs):
    nc = len(clips)
    mine = pl.ds(clips[0] * 2 * TOK, nc * 2 * TOK)
    ql, kl, vl, rq, rk, mass = (ref.at[mine] for ref in refs[:6])
    prob = refs[6].at[:, pl.ds(clips[0] * 4, nc * 4)]
    n32, istd = (ref.at[mine] for ref in refs[7:9])
    w_qkv = refs[9]
    outs = refs[10 : 10 + 4 * nc]
    ext, total, ones4, dqs, dks, dqb, dkb, dvb = refs[10 + 4 * nc :]
    rows = nc * 2 * TOK
    ones4[...] = head_blocks((QW, QW), HEAD_DIM)
    low = low_lanes((TOK, 128))
    upper = lax.broadcasted_iota(jnp.int32, (128, TOK), 0) < HEAD_DIM
    lane = lax.broadcasted_iota(jnp.int32, (1, 128), 1)

    def attend(quad):
        firsts, seconds, thirds, norms = [], [], [], []
        for n, c in enumerate(clips):
            for p in range(2):
                head = quad * 4 + 2 * p
                lanes = slice(quad * QW + p * 128, quad * QW + (p + 1) * 128)
                factor = jnp.where(lane < HEAD_DIM, hscale[head], hscale[head + 1])
                shared = {}
                for w in range(2 * n, 2 * n + 2):
                    at = slice(w * TOK, (w + 1) * TOK)
                    held = {}

                    def first(lanes=lanes, w=w, p=p, c=c, at=at, shared=shared, held=held):
                        if not shared:
                            row = d_out[c : c + 1, lanes].astype(BF16).astype(F32)
                            spread = jnp.transpose(jnp.broadcast_to(row, (TOK, 128)))
                            shared["row"] = row
                            shared["spread"] = jnp.concatenate(
                                [jnp.where(upper, spread, 0.0), jnp.where(upper, 0.0, spread)],
                                axis=1,
                            ).astype(BF16)
                        along = jnp.dot(
                            vl[at, lanes], shared["spread"], preferred_element_type=F32
                        )
                        pt = prob[quad, 2 * w + p]
                        inner = jnp.sum(pt * along, axis=0, keepdims=True)
                        held["ds"] = (pt * (along - inner)).astype(BF16)
                        dvb[at, lanes] = (mass[at, lanes] * shared["row"]).astype(BF16)

                    def second(lanes=lanes, at=at, factor=factor, held=held):
                        ds = held["ds"]
                        dk = jnp.dot(ds, split_heads(ql[at, lanes]), preferred_element_type=F32)
                        dks[at, lanes] = dk * factor
                        held["turned"] = jnp.concatenate(
                            [jnp.transpose(ds[:, :TOK]), jnp.transpose(ds[:, TOK:])], axis=1
                        )

                    def third(lanes=lanes, at=at, factor=factor, held=held):
                        dq = jnp.dot(
                            held["turned"],
                            split_heads(kl[at, lanes]),
                            preferred_element_type=F32,
                        )
                        dqs[at, lanes] = dq * factor

                    firsts.append(first)
                    seconds.append(second)
                    thirds.append(third)
            for w in range(2 * n, 2 * n + 2):
                for part in range(2):

                    def job(w=w, part=part):
                        unit, grad, inverse, done = (
                            (ql, dqs, rq, dqb),
                            (kl, dks, rk, dkb),
                        )[part]
                        at = slice(w * TOK, (w + 1) * TOK)
                        q = slice(quad * QW, (quad + 1) * QW)
                        u = unit[at, q].astype(F32)
                        g = grad[at, q]
                        inner = jnp.dot(
                            (u * g).astype(BF16), ones4[...], preferred_element_type=F32
                        )
                        done[at, q] = ((g - u * inner) * inverse[at, q]).astype(BF16)

                    norms.append(job)
        return staged(firsts, seconds, thirds, lag=2) + norms

    def collect(quad):
        jobs = []
        for part in range(0, D, QW):

            def job(part=part):
                cols = slice(part, part + QW)
                got = None
                for k, grad in enumerate((dqb, dkb, dvb)):
                    term = lax.dot_general(
                        grad[:, quad * QW : (quad + 1) * QW],
                        w_qkv[cols, k * D + quad * QW : k * D + (quad + 1) * QW],
                        NT,
                        preferred_element_type=F32,
                    )
                    got = term if got is None else got + term
                total[:, cols] = got if quad == 0 else total[:, cols] + got

            jobs.append(job)
        return jobs

    for quad in range(QUADS):
        interleave(attend(quad), collect(quad - 1) if quad else [])
    interleave(collect(QUADS - 1))
    for n, c in enumerate(clips):
        s0, s1, s2 = shifts[c, 0], shifts[c, 1], shifts[c, 2]
        off0, off1 = s0 + HALO * c, s1 + HALO * c
        turn = (COLS + s2) % COLS
        base = clip_grad[c : c + 1]

        def cells(half, carry):
            for j in range(2 * WH):
                a, b = 2 * half + j // WH, j % WH
                halves = []
                for w in range(2):
                    start = pl.multiple_of((2 * n + w) * TOK + a * (WH * WW) + b * WW, WW)
                    dn = total[pl.ds(start, WW)]
                    y = n32[pl.ds(start, WW)]
                    inv = istd[pl.ds(start, WW)][:, :1]
                    first = jnp.mean(dn, axis=-1, keepdims=True)
                    second = jnp.mean(dn * y, axis=-1, keepdims=True)
                    halves.append(base + inv * (dn - first - y * second))
                cell = pltpu.roll(jnp.concatenate(halves, axis=0), turn, 0)
                ext[n, a + off0, b + off1] = cell.astype(BF16)
            return carry

        lax.fori_loop(0, WT // 2, cells, 0)
        f, nf, r, nr = OWN[c]
        outs[4 * n][...] = ext[n, f : f + nf, r : r + nr]
        for k in range(3):
            f, nf, r, nr = PIECES[c][k]
            outs[4 * n + 1 + k][...] = ext[n, f : f + nf, r : r + nr]


def backward(clips, shifts, hscale, clip_grad, d_out, stored, w_qkv):
    nc = len(clips)
    n = nc * 2 * TOK
    shapes = ((WT, WH, COLS, D),) + PIECE_SHAPES
    return pl.pallas_call(
        partial(backward_kernel, clips),
        out_shape=[jax.ShapeDtypeStruct(s, BF16) for s in shapes * nc],
        in_specs=[smem(), smem()] + [vmem()] * 12,
        out_specs=[vmem()] * (4 * nc),
        scratch_shapes=[
            pltpu.VMEM((nc, GRID, GRID, COLS, D), BF16),
            pltpu.VMEM((n, D), F32),
            pltpu.VMEM((QW, QW), BF16),
            pltpu.VMEM((n, D), F32),
            pltpu.VMEM((n, D), F32),
            pltpu.VMEM((n, D), BF16),
            pltpu.VMEM((n, D), BF16),
            pltpu.VMEM((n, D), BF16),
        ],
        compiler_params=params(14),
        cost_estimate=pl.CostEstimate(
            flops=2 * n * D * 3 * D, bytes_accessed=16 * 2**20, transcendentals=0
        ),
        name="backward",
    )(shifts, hscale, clip_grad, d_out, *stored, w_qkv)


def merge_kernel(c, shifts, own, a, b, corner, *refs):
    out = refs[-1]
    s0, s1 = shifts[c, 0], shifts[c, 1]
    for f in range(WT):
        for r in range(WH):
            if c == 0:
                far_f, far_r = f < HALO, r < HALO
                gone_f, gone_r = f < s0, r < s1
                at_a, at_b, at_c = (f, r - 1), (f - 1, r), (f, r)
            else:
                far_f, far_r = f >= WT - HALO, r >= WH - HALO
                gone_f, gone_r = f >= WT + s0, r >= WH + s1
                at_a, at_b, at_c = (f - 2, r), (f, r - 2), (f - 2, r - 2)
            value = own[f, r]
            if far_f and 0 <= at_a[1] < 3:
                take = jnp.logical_and(gone_f, jnp.logical_not(gone_r))
                value = jnp.where(take, a[at_a], value)
            if far_r and 0 <= at_b[0] < 3:
                take = jnp.logical_and(jnp.logical_not(gone_f), gone_r)
                value = jnp.where(take, b[at_b], value)
            if far_f and far_r:
                value = jnp.where(jnp.logical_and(gone_f, gone_r), corner[at_c], value)
            out[0, f, r] = value


def merge(clip, shifts, own, got, other=None):
    rest = [] if other is None else [other]
    return pl.pallas_call(
        partial(merge_kernel, clip),
        grid=(1,),
        out_shape=jax.ShapeDtypeStruct((2, WT, WH, COLS, D), BF16),
        in_specs=[smem()] + [vmem()] * 4 + [pl.BlockSpec(memory_space=pl.ANY)] * len(rest),
        out_specs=pl.BlockSpec((1, WT, WH, COLS, D), lambda i: (clip, 0, 0, 0, 0)),
        input_output_aliases={5: 0} if rest else {},
        compiler_params=params(4),
        name="merge",
    )(shifts, own, *got, *rest)


def local(video, shifts, head_scale, w_qkv, w_out, w_emb, text, bucket, bucket_scale):
    tokens = lax.axis_size("tm") * lax.axis_size("space") * WT * WH * COLS
    peers = lax.axis_size("batch")
    pieces = pack(video)
    halo = exchange(pieces[:3], 0, -1) + exchange(pieces[3:], 1, -1)
    w_qkv, video, shifts, head_scale = load(halo[2], w_qkv, video, shifts, head_scale)
    *stored, sums = forward(shifts, head_scale, video, halo, w_qkv)
    spread = share(sums, w_out, w_emb, tokens)
    got = lax.all_to_all(spread, ("tm", "space"), 0, 0)
    packed = embed(got, text, bucket, bucket_scale, peers)
    got = lax.all_to_all(packed, "batch", 0, 0)
    text_grad, loss, clip_grad, d_out = contrast(got, w_emb, w_out)
    parts = []
    for c in range(2):
        mine, *pieces = backward((c,), shifts, head_scale, clip_grad, d_out, stored, w_qkv)
        parts.append((mine, exchange(pieces, c, 1)))
    video_grad = merge(0, shifts, *parts[0])
    video_grad = merge(1, shifts, *parts[1], video_grad)
    return (video_grad, text_grad, loss[0, 0])


def solution(mesh):
    in_specs = (
        P("batch", "tm", "space", None, None),
        P("batch", None),
        P(),
        P(),
        P(),
        P(),
        P("batch", None),
        P("batch", None),
        P(),
    )
    out_specs = (P("batch", "tm", "space", None, None), P("batch", None), P())
    return jax.shard_map(local, mesh=mesh, in_specs=in_specs, out_specs=out_specs, check_vma=False)
```

```python
from functools import partial

import jax
import jax.numpy as jnp
from jax import lax
from jax.experimental import pallas as pl
from jax.experimental.pallas import tpu as pltpu
from jax.sharding import PartitionSpec as P

HEADS = 16
HEAD_DIM = 64
D = 1024
EMB = 768
WT = 4
WH = 4
WW = 8
COLS = 16
HALO = 2
TOK = WT * WH * WW
QUADS = 4
QW = 256

SOFTMAX_TEMP = 0.07
NORM_EPS = 1e-05
QUERY_EPS = 1e-06
EMBED_EPS = 1e-06
LOG2E = 1.4426950408889634
F32 = jnp.float32
BF16 = jnp.bfloat16
MIB = 1024 * 1024

NN = (((1,), (0,)), ((), ()))
NT = (((1,), (1,)), ((), ()))
TN = (((0,), (0,)), ((), ()))

GRID = 6
OWN = ((0, 4, 0, 4), (2, 4, 2, 4))
PIECES = (
    ((4, 2, 1, 3), (1, 3, 4, 2), (4, 2, 4, 2)),
    ((0, 2, 2, 3), (2, 3, 0, 2), (0, 2, 0, 2)),
)
GIVEN = (
    ((0, 2, 1, 3), (1, 3, 0, 2), (0, 2, 0, 2)),
    ((2, 2, 0, 3), (0, 3, 2, 2), (2, 2, 2, 2)),
)
PIECE_SHAPES = tuple((g[1], g[3], COLS, D) for g in GIVEN[0])


def vmem():
    return pl.BlockSpec(memory_space=pltpu.VMEM)


def smem():
    return pl.BlockSpec(memory_space=pltpu.SMEM)


def params(mib):
    return pltpu.CompilerParams(vmem_limit_bytes=mib * MIB)


def pack_kernel(video, *outs):
    for c in range(2):
        for k in range(3):
            f, nf, r, nr = GIVEN[c][k]
            outs[3 * c + k][...] = video[c, f : f + nf, r : r + nr]


def pack(video):
    return pl.pallas_call(
        pack_kernel,
        out_shape=[jax.ShapeDtypeStruct(s, BF16) for s in PIECE_SHAPES * 2],
        in_specs=[vmem()],
        out_specs=[vmem()] * 6,
        compiler_params=params(4),
        name="pack",
    )(video)


def load_kernel(after, w_hbm, video_hbm, shifts, hscale, w_out, video_out, shifts_out, scale_out, sems):
    copies = [
        pltpu.make_async_copy(w_hbm, w_out, sems.at[0]),
        pltpu.make_async_copy(video_hbm, video_out, sems.at[1]),
    ]
    for copy in copies:
        copy.start()
    for c in range(2):
        for k in range(3):
            shifts_out[c, k] = shifts[c, k]
    for h in range(HEADS):
        scale_out[h] = hscale[h]
    for copy in copies:
        copy.wait()


def load(after, w_qkv, video, shifts, hscale):
    return pl.pallas_call(
        load_kernel,
        out_shape=[
            jax.ShapeDtypeStruct(x.shape, x.dtype) for x in (w_qkv, video, shifts, hscale)
        ],
        in_specs=[pl.BlockSpec(memory_space=pl.ANY)] * 3 + [smem()] * 2,
        out_specs=[vmem()] * 2 + [smem()] * 2,
        scratch_shapes=[pltpu.SemaphoreType.DMA((2,))],
        compiler_params=params(4),
        cost_estimate=pl.CostEstimate(
            flops=0, bytes_accessed=2 * (w_qkv.size + video.size), transcendentals=0
        ),
        name="load",
    )(after, w_qkv, video, shifts, hscale)


def exchange(pieces, clip, sign):
    tm, space = lax.axis_size("tm"), lax.axis_size("space")
    step = sign if clip == 0 else -sign
    out = []
    for piece, (dt, ds) in zip(pieces, ((step, 0), (0, step), (step, step))):
        pairs = [
            (t * space + s, ((t + dt) % tm) * space + (s + ds) % space)
            for t in range(tm)
            for s in range(space)
        ]
        out.append(lax.ppermute(piece, ("tm", "space"), pairs))
    return out


def head_blocks(shape, width):
    row = lax.broadcasted_iota(jnp.int32, shape, 0) // width
    lane = lax.broadcasted_iota(jnp.int32, shape, 1) // HEAD_DIM
    return (row == lane).astype(F32).astype(BF16)


def low_lanes(shape):
    return lax.broadcasted_iota(jnp.int32, shape, 1) < HEAD_DIM


def split_heads(pair):
    low = low_lanes((1, 2 * HEAD_DIM)).astype(F32)
    return jnp.concatenate(
        [pair * low.astype(BF16), pair * (1.0 - low).astype(BF16)], axis=0
    )


def window_mask(frame0, row0, col0, s0, s1, s2, frames, rows):
    def label(index):
        f = frame0 + index // (WH * WW) + s0
        r = row0 + (index // WW) % WH + s1
        c = col0 + index % WW + s2
        one = lambda v, n: jnp.where((v < 0) | (v >= n), 1, 0)
        return one(f, frames) * 4 + one(r, rows) * 2 + one(c, COLS)

    key = lax.broadcasted_iota(jnp.int32, (TOK, 1), 0)
    query = lax.broadcasted_iota(jnp.int32, (1, 2 * TOK), 1) % TOK
    return jnp.where(label(key) == label(query), 1.0, 0.0)


def forward_kernel(clips, frames, rows_all, shifts, hscale, video, *refs):
    nc = len(clips)
    frame0 = lax.axis_index("tm") * WT
    row0 = lax.axis_index("space") * WH
    halo, refs = refs[: 3 * nc], refs[3 * nc :]
    w_qkv, refs = refs[0], refs[1:]
    ql, kl, vl, rq, rk, mass, prob, n32, istd, sums = refs[:10]
    ext, xb, masks, ones4, ones2, qs, ks = refs[10:]
    ones4[...] = head_blocks((QW, QW), HEAD_DIM)
    ones2[...] = head_blocks((2 * TOK, 2 * HEAD_DIM), TOK)
    for n, c in enumerate(clips):
        f, nf, r, nr = OWN[c]
        ext[n, f : f + nf, r : r + nr] = video[c]
        for k in range(3):
            f, nf, r, nr = PIECES[c][k]
            ext[n, f : f + nf, r : r + nr] = halo[3 * n + k][...]
        s0, s1, s2 = shifts[c, 0], shifts[c, 1], shifts[c, 2]
        off0, off1 = s0 + HALO * c, s1 + HALO * c
        turn = (COLS - s2) % COLS

        def cells(half, total):
            for j in range(2 * WH):
                a, b = 2 * half + j // WH, j % WH
                x = ext[n, a + off0, b + off1].astype(F32)
                total = total + x
                x = pltpu.roll(x, turn, 0)
                centered = x - jnp.mean(x, axis=-1, keepdims=True)
                inv = lax.rsqrt(
                    jnp.mean(centered * centered, axis=-1, keepdims=True) + NORM_EPS
                )
                y = centered * inv
                wide = jnp.broadcast_to(inv, (COLS, 128))
                for w in range(2):
                    start = pl.multiple_of((2 * n + w) * TOK + a * (WH * WW) + b * WW, WW)
                    n32[pl.ds(start, WW)] = y[w * WW : (w + 1) * WW]
                    istd[pl.ds(start, WW)] = wide[w * WW : (w + 1) * WW]
            return total

        total = jnp.zeros((COLS, D), F32)
        for half in range(WT // 2):
            total = cells(half, total)
        sums[2 * n : 2 * n + 1] = jnp.sum(total, axis=0, keepdims=True)
        for w in range(2):
            masks[2 * n + w] = window_mask(
                frame0, row0, w * WW, s0, s1, s2, frames, rows_all
            )
    xb[...] = n32[...].astype(BF16)
    lane = lax.broadcasted_iota(jnp.int32, (1, 2 * TOK), 1)

    def project(quad):
        jobs = []
        at_quad = slice(quad * QW, (quad + 1) * QW)
        for part in range(3):

            def job(part=part):
                w = w_qkv[:, part * D + quad * QW : part * D + (quad + 1) * QW]
                value = jnp.dot(xb[...], w, preferred_element_type=F32)
                if part == 2:
                    vl[:, at_quad] = value.astype(BF16)
                else:
                    (qs, ks)[part][...] = value

            jobs.append(job)
        for part in range(2):
            for w in range(2 * nc):

                def job(part=part, w=w):
                    at = slice(w * TOK, (w + 1) * TOK)
                    full, unit, inverse = ((qs, ql, rq), (ks, kl, rk))[part]
                    value = full[at]
                    square = jnp.dot(
                        (value * value).astype(BF16), ones4[...], preferred_element_type=F32
                    )
                    inv = lax.rsqrt(square + QUERY_EPS)
                    inverse[at, at_quad] = inv
                    unit[at, at_quad] = (value * inv).astype(BF16)

                jobs.append(job)
        return jobs

    def attend(quad):
        firsts, seconds = [], []
        for p in range(2):
            head = quad * 4 + 2 * p
            lanes = slice(quad * QW + p * 128, quad * QW + (p + 1) * 128)
            for w in range(2 * nc):
                at = slice(w * TOK, (w + 1) * TOK)
                held = {}

                def first(head=head, lanes=lanes, w=w, at=at, p=p, held=held):
                    factor = jnp.where(lane < TOK, hscale[head], hscale[head + 1]) * LOG2E
                    score = lax.dot_general(
                        kl[at, lanes], split_heads(ql[at, lanes]), NT, preferred_element_type=F32
                    )
                    e = jnp.exp2(score * factor) * masks[w]
                    held["e"] = e
                    held["inv"] = 1.0 / jnp.sum(e, axis=0, keepdims=True)

                def second(lanes=lanes, w=w, at=at, p=p, held=held):
                    pt = held["e"] * held["inv"]
                    prob[quad, 2 * w + p] = pt
                    mass_here = jnp.dot(pt.astype(BF16), ones2[...], preferred_element_type=F32)
                    mass[at, lanes] = mass_here
                    gathered = jnp.sum(
                        mass_here * vl[at, lanes].astype(F32), axis=0, keepdims=True
                    )
                    row = slice(w // 2 * 2 + 1, w // 2 * 2 + 2)
                    if w % 2:
                        sums[row, lanes] = sums[row, lanes] + gathered
                    else:
                        sums[row, lanes] = gathered

                firsts.append(first)
                seconds.append(second)
        return firsts, seconds

    units = 4 * nc
    plan = spread_jobs(project(0), -1, 0)
    for quad in range(QUADS):
        start = quad * units
        for depth, stage in enumerate(attend(quad)):
            plan += spread_jobs(stage, start + depth * LAG_F, start + depth * LAG_F + units)
        if quad + 1 < QUADS:
            plan += spread_jobs(project(quad + 1), start, start + units - 0.1)
    emit(plan)


LAG_F = 3
LAG_B = 2


def spread_jobs(jobs, start, end):
    step = (end - start) / len(jobs)
    return [(start + k * step, job) for k, job in enumerate(jobs)]


def emit(plan):
    for _, job in sorted(plan, key=lambda item: item[0]):
        job()


def forward(shifts, hscale, video, halo, w_qkv):
    clips = (0, 1)
    nc = len(clips)
    n = nc * 2 * TOK
    frames = lax.axis_size("tm") * WT
    rows_all = lax.axis_size("space") * WH
    return pl.pallas_call(
        partial(forward_kernel, clips, frames, rows_all),
        out_shape=[jax.ShapeDtypeStruct((n, D), BF16)] * 3
        + [jax.ShapeDtypeStruct((n, D), F32)] * 3
        + [
            jax.ShapeDtypeStruct((QUADS, 4 * nc, TOK, 2 * TOK), F32),
            jax.ShapeDtypeStruct((n, D), F32),
            jax.ShapeDtypeStruct((n, 128), F32),
            jax.ShapeDtypeStruct((2 * nc, D), F32),
        ],
        in_specs=[smem(), smem()] + [vmem()] * (2 + 3 * nc),
        out_specs=[vmem()] * 10,
        scratch_shapes=[
            pltpu.VMEM((nc, GRID, GRID, COLS, D), BF16),
            pltpu.VMEM((n, D), BF16),
            pltpu.VMEM((2 * nc, TOK, 2 * TOK), F32),
            pltpu.VMEM((QW, QW), BF16),
            pltpu.VMEM((2 * TOK, 2 * HEAD_DIM), BF16),
            pltpu.VMEM((n, QW), F32),
            pltpu.VMEM((n, QW), F32),
        ],
        compiler_params=params(12),
        cost_estimate=pl.CostEstimate(
            flops=2 * n * D * 3 * D, bytes_accessed=12 * 2**20, transcendentals=n * 2048
        ),
        name="forward",
    )(shifts, hscale, video, *halo, w_qkv)


def share_kernel(tokens, sums, w_out, w_emb, out):
    means = sums[...] / tokens
    pooled = jnp.concatenate([means[0:1], means[2:3]], axis=0) + full_dot(
        jnp.concatenate([means[1:2], means[3:4]], axis=0), w_out[...], NN
    )
    block = full_dot(pooled, w_emb[...], NN)
    for peer in range(out.shape[0]):
        out[peer] = block


def share(sums, w_out, w_emb, tokens):
    plane = lax.axis_size("tm") * lax.axis_size("space")
    return pl.pallas_call(
        partial(share_kernel, tokens),
        out_shape=jax.ShapeDtypeStruct((plane, 2, EMB), F32),
        in_specs=[vmem()] * 3,
        out_specs=vmem(),
        compiler_params=params(4),
        name="share",
    )(sums, w_out, w_emb)


def embed_kernel(got, text, bucket, levels, out):
    embedded = jnp.sum(got[...], axis=0)
    held = bucket[...]
    weight = jnp.zeros(held.shape, F32)
    for level in range(levels.shape[0]):
        weight = weight + jnp.where(held == level, levels[level], 0.0)
    weight = jnp.concatenate(
        [weight, jnp.zeros((held.shape[0], 128 - held.shape[1]), F32)], axis=1
    )
    words = text[...].astype(F32)
    block = jnp.concatenate(
        [
            jnp.concatenate([embedded, weight], axis=1),
            jnp.concatenate([words, jnp.zeros_like(weight)], axis=1),
        ],
        axis=0,
    )
    for peer in range(out.shape[0]):
        out[peer] = block


def embed(got, text, bucket, levels, peers):
    return pl.pallas_call(
        embed_kernel,
        out_shape=jax.ShapeDtypeStruct((peers, 4, EMB + 128), F32),
        in_specs=[vmem()] * 3 + [smem()],
        out_specs=vmem(),
        compiler_params=params(4),
        name="embed",
    )(got, text, bucket, levels)


def three_parts(wide):
    high = wide.astype(BF16)
    rest = wide - high.astype(F32)
    middle = rest.astype(BF16)
    low = (rest - middle.astype(F32)).astype(BF16)
    return jnp.concatenate([high, middle, low], axis=0)


def full_dot(wide, weight, dims):
    n = wide.shape[0]
    got = lax.dot_general(three_parts(wide), weight, dims, preferred_element_type=F32)
    return got[:n] + got[n : 2 * n] + got[2 * n :]


def contrast_kernel(got, w_emb, w_out, text_grad, loss, clip_grad, d_out):
    peers = got.shape[0]
    n = 2 * peers
    first_clip = 2 * lax.axis_index("batch")
    embedded = jnp.concatenate([got[p, 0:2, :EMB] for p in range(peers)], axis=0)
    weights = jnp.concatenate([got[p, 0:2, EMB:] for p in range(peers)], axis=0)[:, :n]
    words = jnp.concatenate([got[p, 2:4, :EMB] for p in range(peers)], axis=0)
    clip_norm = jnp.sqrt(jnp.sum(embedded * embedded, axis=-1, keepdims=True) + EMBED_EPS)
    text_norm = jnp.sqrt(jnp.sum(words * words, axis=-1, keepdims=True) + EMBED_EPS)
    clip_unit = embedded / clip_norm
    text_unit = words / text_norm
    exact = lax.Precision.HIGHEST
    logits = (
        lax.dot_general(clip_unit, text_unit, NT, precision=exact, preferred_element_type=F32)
        / SOFTMAX_TEMP
    )
    own = lax.broadcasted_iota(jnp.int32, (n, n), 0) == lax.broadcasted_iota(
        jnp.int32, (n, n), 1
    )
    exp_logit = jnp.exp(logits)
    other = jnp.where(own, 0.0, weights)
    negative = other * exp_logit
    diagonal = jnp.where(own, logits, 0.0)
    row_self = jnp.sum(diagonal, axis=1, keepdims=True)
    col_self = jnp.sum(diagonal, axis=0, keepdims=True)
    row_weight = jnp.sum(other, axis=1, keepdims=True)
    col_weight = jnp.sum(other, axis=0, keepdims=True)
    row_part = (
        jnp.exp(row_self) + (n - 1) * jnp.sum(negative, axis=1, keepdims=True) / row_weight
    )
    col_part = (
        jnp.exp(col_self) + (n - 1) * jnp.sum(negative, axis=0, keepdims=True) / col_weight
    )
    summed = jnp.sum(jnp.log(row_part) - row_self, axis=0, keepdims=True) + jnp.sum(
        jnp.log(col_part) - col_self, axis=1, keepdims=True
    )
    loss[...] = summed / (2 * n)
    scaled = (n - 1) * weights * exp_logit
    off = scaled * (1.0 / (row_weight * row_part)) + scaled * (1.0 / (col_weight * col_part))
    on = exp_logit / row_part - 1.0 + exp_logit / col_part - 1.0
    grad = jnp.where(own, on, off)
    d_clip = (
        jnp.dot(grad, text_unit, precision=exact, preferred_element_type=F32) / SOFTMAX_TEMP
    )
    d_text = (
        lax.dot_general(grad, clip_unit, TN, precision=exact, preferred_element_type=F32)
        / SOFTMAX_TEMP
    )
    text_all = (
        d_text - text_unit * jnp.sum(text_unit * d_text, axis=-1, keepdims=True)
    ) / text_norm
    embed_all = (
        d_clip - clip_unit * jnp.sum(clip_unit * d_clip, axis=-1, keepdims=True)
    ) / clip_norm
    row = lax.broadcasted_iota(jnp.int32, (n, 1), 0)

    def mine(array):
        return jnp.concatenate(
            [
                jnp.sum(
                    jnp.where(row == first_clip + c, array, 0.0), axis=0, keepdims=True
                )
                for c in range(2)
            ],
            axis=0,
        )

    text_grad[...] = mine(text_all)
    pooled_grad = full_dot(mine(embed_all), w_emb[...], NT)
    clip_grad[...] = pooled_grad
    d_out[...] = full_dot(pooled_grad, w_out[...], NT)


def contrast(got, w_emb, w_out):
    return pl.pallas_call(
        contrast_kernel,
        out_shape=[
            jax.ShapeDtypeStruct((2, EMB), F32),
            jax.ShapeDtypeStruct((1, 1), F32),
            jax.ShapeDtypeStruct((2, D), F32),
            jax.ShapeDtypeStruct((2, D), F32),
        ],
        in_specs=[vmem()] * 3,
        out_specs=[vmem()] * 4,
        compiler_params=params(4),
        name="contrast",
    )(got, w_emb, w_out)


def backward_kernel(clips, shifts, hscale, clip_grad, d_out, *refs):
    nc = len(clips)
    mine = pl.ds(clips[0] * 2 * TOK, nc * 2 * TOK)
    ql, kl, vl, rq, rk, mass = (ref.at[mine] for ref in refs[:6])
    prob = refs[6].at[:, pl.ds(clips[0] * 4, nc * 4)]
    n32, istd = (ref.at[mine] for ref in refs[7:9])
    w_qkv = refs[9]
    outs = refs[10 : 10 + 4 * nc]
    ext, total, ones4, dqs, dks, dqb, dkb, dvb = refs[10 + 4 * nc :]
    rows = nc * 2 * TOK
    ones4[...] = head_blocks((QW, QW), HEAD_DIM)
    low = low_lanes((TOK, 128))
    upper = lax.broadcasted_iota(jnp.int32, (128, TOK), 0) < HEAD_DIM
    lane = lax.broadcasted_iota(jnp.int32, (1, 128), 1)

    def attend(quad):
        firsts, seconds, thirds, norms = [], [], [], []
        for n, c in enumerate(clips):
            for p in range(2):
                head = quad * 4 + 2 * p
                lanes = slice(quad * QW + p * 128, quad * QW + (p + 1) * 128)
                factor = jnp.where(lane < HEAD_DIM, hscale[head], hscale[head + 1])
                shared = {}
                for w in range(2 * n, 2 * n + 2):
                    at = slice(w * TOK, (w + 1) * TOK)
                    held = {}

                    def first(lanes=lanes, w=w, p=p, c=c, at=at, shared=shared, held=held):
                        if not shared:
                            row = d_out[c : c + 1, lanes].astype(BF16).astype(F32)
                            spread = jnp.transpose(jnp.broadcast_to(row, (TOK, 128)))
                            shared["row"] = row
                            shared["spread"] = jnp.concatenate(
                                [jnp.where(upper, spread, 0.0), jnp.where(upper, 0.0, spread)],
                                axis=1,
                            ).astype(BF16)
                        along = jnp.dot(
                            vl[at, lanes], shared["spread"], preferred_element_type=F32
                        )
                        pt = prob[quad, 2 * w + p]
                        inner = jnp.sum(pt * along, axis=0, keepdims=True)
                        held["ds"] = (pt * (along - inner)).astype(BF16)
                        dvb[at, lanes] = (mass[at, lanes] * shared["row"]).astype(BF16)

                    def second(lanes=lanes, at=at, factor=factor, held=held):
                        ds = held["ds"]
                        dk = jnp.dot(ds, split_heads(ql[at, lanes]), preferred_element_type=F32)
                        dks[at, lanes] = dk * factor
                        held["turned"] = jnp.concatenate(
                            [jnp.transpose(ds[:, :TOK]), jnp.transpose(ds[:, TOK:])], axis=1
                        )

                    def third(lanes=lanes, at=at, factor=factor, held=held):
                        dq = jnp.dot(
                            held["turned"],
                            split_heads(kl[at, lanes]),
                            preferred_element_type=F32,
                        )
                        dqs[at, lanes] = dq * factor

                    firsts.append(first)
                    seconds.append(second)
                    thirds.append(third)
            for w in range(2 * n, 2 * n + 2):
                for part in range(2):

                    def job(w=w, part=part):
                        unit, grad, inverse, done = (
                            (ql, dqs, rq, dqb),
                            (kl, dks, rk, dkb),
                        )[part]
                        at = slice(w * TOK, (w + 1) * TOK)
                        q = slice(quad * QW, (quad + 1) * QW)
                        u = unit[at, q].astype(F32)
                        g = grad[at, q]
                        inner = jnp.dot(
                            (u * g).astype(BF16), ones4[...], preferred_element_type=F32
                        )
                        done[at, q] = ((g - u * inner) * inverse[at, q]).astype(BF16)

                    norms.append(job)
        return firsts, seconds, thirds, norms

    def collect(quad):
        jobs = []
        for part in range(0, D, QW):

            def job(part=part):
                cols = slice(part, part + QW)
                got = None
                for k, grad in enumerate((dqb, dkb, dvb)):
                    term = lax.dot_general(
                        grad[:, quad * QW : (quad + 1) * QW],
                        w_qkv[cols, k * D + quad * QW : k * D + (quad + 1) * QW],
                        NT,
                        preferred_element_type=F32,
                    )
                    got = term if got is None else got + term
                total[:, cols] = got if quad == 0 else total[:, cols] + got

            jobs.append(job)
        return jobs

    units = 4 * nc
    plan = []
    for quad in range(QUADS):
        *stages, norms = attend(quad)
        start = quad * units
        for depth, stage in enumerate(stages):
            plan += spread_jobs(stage, start + depth * LAG_B, start + depth * LAG_B + units)
        done = start + 2 * LAG_B + units - 0.9
        plan += spread_jobs(norms, done, done + 1)
        plan += spread_jobs(collect(quad), done + 1, done + 1 + units)
    emit(plan)
    for n, c in enumerate(clips):
        s0, s1, s2 = shifts[c, 0], shifts[c, 1], shifts[c, 2]
        off0, off1 = s0 + HALO * c, s1 + HALO * c
        turn = (COLS + s2) % COLS
        base = clip_grad[c : c + 1]

        def cells(half):
            for j in range(2 * WH):
                a, b = 2 * half + j // WH, j % WH
                halves = []
                for w in range(2):
                    start = pl.multiple_of((2 * n + w) * TOK + a * (WH * WW) + b * WW, WW)
                    dn = total[pl.ds(start, WW)]
                    y = n32[pl.ds(start, WW)]
                    inv = istd[pl.ds(start, WW)][:, :1]
                    first = jnp.mean(dn, axis=-1, keepdims=True)
                    second = jnp.mean(dn * y, axis=-1, keepdims=True)
                    halves.append(base + inv * (dn - first - y * second))
                cell = pltpu.roll(jnp.concatenate(halves, axis=0), turn, 0)
                ext[n, a + off0, b + off1] = cell.astype(BF16)

        for half in range(WT // 2):
            cells(half)
        f, nf, r, nr = OWN[c]
        outs[4 * n][...] = ext[n, f : f + nf, r : r + nr]
        for k in range(3):
            f, nf, r, nr = PIECES[c][k]
            outs[4 * n + 1 + k][...] = ext[n, f : f + nf, r : r + nr]


def backward(clips, shifts, hscale, clip_grad, d_out, stored, w_qkv):
    nc = len(clips)
    n = nc * 2 * TOK
    shapes = ((WT, WH, COLS, D),) + PIECE_SHAPES
    return pl.pallas_call(
        partial(backward_kernel, clips),
        out_shape=[jax.ShapeDtypeStruct(s, BF16) for s in shapes * nc],
        in_specs=[smem(), smem()] + [vmem()] * 12,
        out_specs=[vmem()] * (4 * nc),
        scratch_shapes=[
            pltpu.VMEM((nc, GRID, GRID, COLS, D), BF16),
            pltpu.VMEM((n, D), F32),
            pltpu.VMEM((QW, QW), BF16),
            pltpu.VMEM((n, D), F32),
            pltpu.VMEM((n, D), F32),
            pltpu.VMEM((n, D), BF16),
            pltpu.VMEM((n, D), BF16),
            pltpu.VMEM((n, D), BF16),
        ],
        compiler_params=params(14),
        cost_estimate=pl.CostEstimate(
            flops=2 * n * D * 3 * D, bytes_accessed=16 * 2**20, transcendentals=0
        ),
        name="backward",
    )(shifts, hscale, clip_grad, d_out, *stored, w_qkv)


def merge_kernel(c, shifts, own, a, b, corner, *refs):
    out = refs[-1]
    s0, s1 = shifts[c, 0], shifts[c, 1]
    for f in range(WT):
        for r in range(WH):
            if c == 0:
                far_f, far_r = f < HALO, r < HALO
                gone_f, gone_r = f < s0, r < s1
                at_a, at_b, at_c = (f, r - 1), (f - 1, r), (f, r)
            else:
                far_f, far_r = f >= WT - HALO, r >= WH - HALO
                gone_f, gone_r = f >= WT + s0, r >= WH + s1
                at_a, at_b, at_c = (f - 2, r), (f, r - 2), (f - 2, r - 2)
            value = own[f, r]
            if far_f and 0 <= at_a[1] < 3:
                take = jnp.logical_and(gone_f, jnp.logical_not(gone_r))
                value = jnp.where(take, a[at_a], value)
            if far_r and 0 <= at_b[0] < 3:
                take = jnp.logical_and(jnp.logical_not(gone_f), gone_r)
                value = jnp.where(take, b[at_b], value)
            if far_f and far_r:
                value = jnp.where(jnp.logical_and(gone_f, gone_r), corner[at_c], value)
            out[0, f, r] = value


def merge(clip, shifts, own, got, other=None):
    rest = [] if other is None else [other]
    return pl.pallas_call(
        partial(merge_kernel, clip),
        grid=(1,),
        out_shape=jax.ShapeDtypeStruct((2, WT, WH, COLS, D), BF16),
        in_specs=[smem()] + [vmem()] * 4 + [pl.BlockSpec(memory_space=pl.ANY)] * len(rest),
        out_specs=pl.BlockSpec((1, WT, WH, COLS, D), lambda i: (clip, 0, 0, 0, 0)),
        input_output_aliases={5: 0} if rest else {},
        compiler_params=params(4),
        name="merge",
    )(shifts, own, *got, *rest)


def local(video, shifts, head_scale, w_qkv, w_out, w_emb, text, bucket, bucket_scale):
    tokens = lax.axis_size("tm") * lax.axis_size("space") * WT * WH * COLS
    peers = lax.axis_size("batch")
    pieces = pack(video)
    halo = exchange(pieces[:3], 0, -1) + exchange(pieces[3:], 1, -1)
    w_qkv, video, shifts, head_scale = load(halo[2], w_qkv, video, shifts, head_scale)
    *stored, sums = forward(shifts, head_scale, video, halo, w_qkv)
    spread = share(sums, w_out, w_emb, tokens)
    got = lax.all_to_all(spread, ("tm", "space"), 0, 0)
    packed = embed(got, text, bucket, bucket_scale, peers)
    got = lax.all_to_all(packed, "batch", 0, 0)
    text_grad, loss, clip_grad, d_out = contrast(got, w_emb, w_out)
    parts = []
    for c in range(2):
        mine, *pieces = backward((c,), shifts, head_scale, clip_grad, d_out, stored, w_qkv)
        parts.append((mine, exchange(pieces, c, 1)))
    video_grad = merge(0, shifts, *parts[0])
    video_grad = merge(1, shifts, *parts[1], video_grad)
    return (video_grad, text_grad, loss[0, 0])


def solution(mesh):
    in_specs = (
        P("batch", "tm", "space", None, None),
        P("batch", None),
        P(),
        P(),
        P(),
        P(),
        P("batch", None),
        P("batch", None),
        P(),
    )
    out_specs = (P("batch", "tm", "space", None, None), P("batch", None), P())
    return jax.shard_map(local, mesh=mesh, in_specs=in_specs, out_specs=out_specs, check_vma=False)
```

```python
from functools import partial

import jax
import jax.numpy as jnp
from jax import lax
from jax.experimental import pallas as pl
from jax.experimental.pallas import tpu as pltpu
from jax.sharding import PartitionSpec as P

HEADS = 16
HEAD_DIM = 64
D = 1024
EMB = 768
WT = 4
WH = 4
WW = 8
COLS = 16
HALO = 2
TOK = WT * WH * WW
QUADS = 4
QW = 256

SOFTMAX_TEMP = 0.07
NORM_EPS = 1e-05
QUERY_EPS = 1e-06
EMBED_EPS = 1e-06
LOG2E = 1.4426950408889634
F32 = jnp.float32
BF16 = jnp.bfloat16
MIB = 1024 * 1024

NN = (((1,), (0,)), ((), ()))
NT = (((1,), (1,)), ((), ()))
TN = (((0,), (0,)), ((), ()))

GRID = 6
OWN = ((0, 4, 0, 4), (2, 4, 2, 4))
PIECES = (
    ((4, 2, 1, 3), (1, 3, 4, 2), (4, 2, 4, 2)),
    ((0, 2, 2, 3), (2, 3, 0, 2), (0, 2, 0, 2)),
)
GIVEN = (
    ((0, 2, 1, 3), (1, 3, 0, 2), (0, 2, 0, 2)),
    ((2, 2, 0, 3), (0, 3, 2, 2), (2, 2, 2, 2)),
)
PIECE_SHAPES = tuple((g[1], g[3], COLS, D) for g in GIVEN[0])


def vmem():
    return pl.BlockSpec(memory_space=pltpu.VMEM)


def smem():
    return pl.BlockSpec(memory_space=pltpu.SMEM)


def params(mib):
    return pltpu.CompilerParams(vmem_limit_bytes=mib * MIB)


def pack_kernel(video, *outs):
    for c in range(2):
        for k in range(3):
            f, nf, r, nr = GIVEN[c][k]
            outs[3 * c + k][...] = video[c, f : f + nf, r : r + nr]
    outs[6][...] = video[...]


def pack(video):
    return pl.pallas_call(
        pack_kernel,
        out_shape=[jax.ShapeDtypeStruct(s, BF16) for s in PIECE_SHAPES * 2 + (video.shape,)],
        in_specs=[vmem()],
        out_specs=[vmem()] * 7,
        compiler_params=params(4),
        name="pack",
    )(video)


def load_kernel(after, w_hbm, w_out, sem):
    copy = pltpu.make_async_copy(w_hbm, w_out, sem)
    copy.start()
    copy.wait()


def load(after, w_qkv):
    anywhere = pl.BlockSpec(memory_space=pl.ANY)
    return pl.pallas_call(
        load_kernel,
        out_shape=jax.ShapeDtypeStruct(w_qkv.shape, w_qkv.dtype),
        in_specs=[anywhere] * 2,
        out_specs=vmem(),
        scratch_shapes=[pltpu.SemaphoreType.DMA],
        compiler_params=params(4),
        cost_estimate=pl.CostEstimate(
            flops=0, bytes_accessed=4 * w_qkv.size, transcendentals=0
        ),
        name="load",
    )(after, w_qkv)


def shift_of(small, clip):
    return tuple(small[1 + clip, k].astype(jnp.int32) for k in range(3))


def exchange(pieces, clip, sign):
    tm, space = lax.axis_size("tm"), lax.axis_size("space")
    step = sign if clip == 0 else -sign
    out = []
    for piece, (dt, ds) in zip(pieces, ((step, 0), (0, step), (step, step))):
        pairs = [
            (t * space + s, ((t + dt) % tm) * space + (s + ds) % space)
            for t in range(tm)
            for s in range(space)
        ]
        out.append(lax.ppermute(piece, ("tm", "space"), pairs))
    return out


def head_blocks(shape, width):
    row = lax.broadcasted_iota(jnp.int32, shape, 0) // width
    lane = lax.broadcasted_iota(jnp.int32, shape, 1) // HEAD_DIM
    return (row == lane).astype(F32).astype(BF16)


def low_lanes(shape):
    return lax.broadcasted_iota(jnp.int32, shape, 1) < HEAD_DIM


def split_heads(pair):
    low = low_lanes((1, 2 * HEAD_DIM)).astype(F32)
    return jnp.concatenate(
        [pair * low.astype(BF16), pair * (1.0 - low).astype(BF16)], axis=0
    )


def window_mask(frame0, row0, col0, s0, s1, s2, frames, rows):
    def label(index):
        f = frame0 + index // (WH * WW) + s0
        r = row0 + (index // WW) % WH + s1
        c = col0 + index % WW + s2
        one = lambda v, n: jnp.where((v < 0) | (v >= n), 1, 0)
        return one(f, frames) * 4 + one(r, rows) * 2 + one(c, COLS)

    key = lax.broadcasted_iota(jnp.int32, (TOK, 1), 0)
    query = lax.broadcasted_iota(jnp.int32, (1, 2 * TOK), 1) % TOK
    return jnp.where(label(key) == label(query), 1.0, 0.0)


def forward_kernel(clips, frames, rows_all, small, video, *refs):
    nc = len(clips)
    frame0 = lax.axis_index("tm") * WT
    row0 = lax.axis_index("space") * WH
    halo, refs = refs[: 3 * nc], refs[3 * nc :]
    w_qkv, refs = refs[0], refs[1:]
    ql, kl, vl, rq, rk, mass, prob, n32, istd, sums = refs[:10]
    ext, xb, masks, ones4, ones2, qs, ks = refs[10:]
    ones4[...] = head_blocks((QW, QW), HEAD_DIM)
    ones2[...] = head_blocks((2 * TOK, 2 * HEAD_DIM), TOK)
    for n, c in enumerate(clips):
        f, nf, r, nr = OWN[c]
        ext[n, f : f + nf, r : r + nr] = video[c]
        for k in range(3):
            f, nf, r, nr = PIECES[c][k]
            ext[n, f : f + nf, r : r + nr] = halo[3 * n + k][...]
        s0, s1, s2 = shift_of(small, c)
        off0, off1 = s0 + HALO * c, s1 + HALO * c
        turn = (COLS - s2) % COLS

        def cells(half, total):
            for j in range(2 * WH):
                a, b = 2 * half + j // WH, j % WH
                x = ext[n, a + off0, b + off1].astype(F32)
                total = total + x
                x = pltpu.roll(x, turn, 0)
                centered = x - jnp.mean(x, axis=-1, keepdims=True)
                inv = lax.rsqrt(
                    jnp.mean(centered * centered, axis=-1, keepdims=True) + NORM_EPS
                )
                y = centered * inv
                wide = jnp.broadcast_to(inv, (COLS, 128))
                for w in range(2):
                    start = pl.multiple_of((2 * n + w) * TOK + a * (WH * WW) + b * WW, WW)
                    n32[pl.ds(start, WW)] = y[w * WW : (w + 1) * WW]
                    istd[pl.ds(start, WW)] = wide[w * WW : (w + 1) * WW]
            return total

        total = jnp.zeros((COLS, D), F32)
        for half in range(WT // 2):
            total = cells(half, total)
        sums[2 * n : 2 * n + 1] = jnp.sum(total, axis=0, keepdims=True)
        for w in range(2):
            masks[2 * n + w] = window_mask(
                frame0, row0, w * WW, s0, s1, s2, frames, rows_all
            )
    xb[...] = n32[...].astype(BF16)
    lane = lax.broadcasted_iota(jnp.int32, (1, 2 * TOK), 1)

    def project(quad):
        jobs = []
        at_quad = slice(quad * QW, (quad + 1) * QW)
        for part in range(3):

            def job(part=part):
                w = w_qkv[:, part * D + quad * QW : part * D + (quad + 1) * QW]
                value = jnp.dot(xb[...], w, preferred_element_type=F32)
                if part == 2:
                    vl[:, at_quad] = value.astype(BF16)
                else:
                    (qs, ks)[part][...] = value

            jobs.append(job)
        for part in range(2):
            for w in range(2 * nc):

                def job(part=part, w=w):
                    at = slice(w * TOK, (w + 1) * TOK)
                    full, unit, inverse = ((qs, ql, rq), (ks, kl, rk))[part]
                    value = full[at]
                    square = jnp.dot(
                        (value * value).astype(BF16), ones4[...], preferred_element_type=F32
                    )
                    inv = lax.rsqrt(square + QUERY_EPS)
                    inverse[at, at_quad] = inv
                    unit[at, at_quad] = (value * inv).astype(BF16)

                jobs.append(job)
        return jobs

    def attend(quad):
        firsts, seconds = [], []
        for p in range(2):
            head = quad * 4 + 2 * p
            lanes = slice(quad * QW + p * 128, quad * QW + (p + 1) * 128)
            for w in range(2 * nc):
                at = slice(w * TOK, (w + 1) * TOK)
                held = {}

                def first(head=head, lanes=lanes, w=w, at=at, p=p, held=held):
                    factor = jnp.where(lane < TOK, small[0, head], small[0, head + 1]) * LOG2E
                    score = lax.dot_general(
                        kl[at, lanes], split_heads(ql[at, lanes]), NT, preferred_element_type=F32
                    )
                    e = jnp.exp2(score * factor) * masks[w]
                    held["e"] = e
                    held["inv"] = 1.0 / jnp.sum(e, axis=0, keepdims=True)

                def second(lanes=lanes, w=w, at=at, p=p, held=held):
                    pt = held["e"] * held["inv"]
                    prob[quad, 2 * w + p] = pt
                    mass_here = jnp.dot(pt.astype(BF16), ones2[...], preferred_element_type=F32)
                    mass[at, lanes] = mass_here
                    gathered = jnp.sum(
                        mass_here * vl[at, lanes].astype(F32), axis=0, keepdims=True
                    )
                    row = slice(w // 2 * 2 + 1, w // 2 * 2 + 2)
                    if w % 2:
                        sums[row, lanes] = sums[row, lanes] + gathered
                    else:
                        sums[row, lanes] = gathered

                firsts.append(first)
                seconds.append(second)
        return firsts, seconds

    units = 4 * nc
    plan = spread_jobs(project(0), -1, 0)
    for quad in range(QUADS):
        start = quad * units
        for depth, stage in enumerate(attend(quad)):
            plan += spread_jobs(stage, start + depth * LAG_F, start + depth * LAG_F + units)
        if quad + 1 < QUADS:
            plan += spread_jobs(project(quad + 1), start, start + units - 0.1)
    emit(plan)


LAG_F = 3
LAG_B = 2


def spread_jobs(jobs, start, end):
    step = (end - start) / len(jobs)
    return [(start + k * step, job) for k, job in enumerate(jobs)]


def emit(plan):
    for _, job in sorted(plan, key=lambda item: item[0]):
        job()


def forward(small, video, halo, w_qkv):
    clips = (0, 1)
    nc = len(clips)
    n = nc * 2 * TOK
    frames = lax.axis_size("tm") * WT
    rows_all = lax.axis_size("space") * WH
    return pl.pallas_call(
        partial(forward_kernel, clips, frames, rows_all),
        out_shape=[jax.ShapeDtypeStruct((n, D), BF16)] * 3
        + [jax.ShapeDtypeStruct((n, D), F32)] * 3
        + [
            jax.ShapeDtypeStruct((QUADS, 4 * nc, TOK, 2 * TOK), F32),
            jax.ShapeDtypeStruct((n, D), F32),
            jax.ShapeDtypeStruct((n, 128), F32),
            jax.ShapeDtypeStruct((2 * nc, D), F32),
        ],
        in_specs=[smem()] + [vmem()] * (2 + 3 * nc),
        out_specs=[vmem()] * 10,
        scratch_shapes=[
            pltpu.VMEM((nc, GRID, GRID, COLS, D), BF16),
            pltpu.VMEM((n, D), BF16),
            pltpu.VMEM((2 * nc, TOK, 2 * TOK), F32),
            pltpu.VMEM((QW, QW), BF16),
            pltpu.VMEM((2 * TOK, 2 * HEAD_DIM), BF16),
            pltpu.VMEM((n, QW), F32),
            pltpu.VMEM((n, QW), F32),
        ],
        compiler_params=params(12),
        cost_estimate=pl.CostEstimate(
            flops=2 * n * D * 3 * D, bytes_accessed=12 * 2**20, transcendentals=n * 2048
        ),
        name="forward",
    )(small, video, *halo, w_qkv)


def share_kernel(tokens, sums, w_out, w_emb, out):
    means = sums[...] / tokens
    pooled = jnp.concatenate([means[0:1], means[2:3]], axis=0) + full_dot(
        jnp.concatenate([means[1:2], means[3:4]], axis=0), w_out[...], NN
    )
    block = full_dot(pooled, w_emb[...], NN)
    for peer in range(out.shape[0]):
        out[peer] = block


def share(sums, w_out, w_emb, tokens):
    plane = lax.axis_size("tm") * lax.axis_size("space")
    return pl.pallas_call(
        partial(share_kernel, tokens),
        out_shape=jax.ShapeDtypeStruct((plane, 2, EMB), F32),
        in_specs=[vmem()] * 3,
        out_specs=vmem(),
        compiler_params=params(4),
        name="share",
    )(sums, w_out, w_emb)


def embed_kernel(got, text, bucket, levels, out):
    embedded = jnp.sum(got[...], axis=0)
    held = bucket[...]
    weight = jnp.zeros(held.shape, F32)
    for level in range(levels.shape[0]):
        weight = weight + jnp.where(held == level, levels[level], 0.0)
    weight = jnp.concatenate(
        [weight, jnp.zeros((held.shape[0], 128 - held.shape[1]), F32)], axis=1
    )
    words = text[...].astype(F32)
    block = jnp.concatenate(
        [
            jnp.concatenate([embedded, weight], axis=1),
            jnp.concatenate([words, jnp.zeros_like(weight)], axis=1),
        ],
        axis=0,
    )
    for peer in range(out.shape[0]):
        out[peer] = block


def embed(got, text, bucket, levels, peers):
    return pl.pallas_call(
        embed_kernel,
        out_shape=jax.ShapeDtypeStruct((peers, 4, EMB + 128), F32),
        in_specs=[vmem()] * 3 + [smem()],
        out_specs=vmem(),
        compiler_params=params(4),
        name="embed",
    )(got, text, bucket, levels)


def three_parts(wide):
    high = wide.astype(BF16)
    rest = wide - high.astype(F32)
    middle = rest.astype(BF16)
    low = (rest - middle.astype(F32)).astype(BF16)
    return jnp.concatenate([high, middle, low], axis=0)


def full_dot(wide, weight, dims):
    n = wide.shape[0]
    got = lax.dot_general(three_parts(wide), weight, dims, preferred_element_type=F32)
    return got[:n] + got[n : 2 * n] + got[2 * n :]


def contrast_kernel(got, w_emb, w_out, text_grad, loss, clip_grad, d_out):
    peers = got.shape[0]
    n = 2 * peers
    first_clip = 2 * lax.axis_index("batch")
    embedded = jnp.concatenate([got[p, 0:2, :EMB] for p in range(peers)], axis=0)
    weights = jnp.concatenate([got[p, 0:2, EMB:] for p in range(peers)], axis=0)[:, :n]
    words = jnp.concatenate([got[p, 2:4, :EMB] for p in range(peers)], axis=0)
    clip_norm = jnp.sqrt(jnp.sum(embedded * embedded, axis=-1, keepdims=True) + EMBED_EPS)
    text_norm = jnp.sqrt(jnp.sum(words * words, axis=-1, keepdims=True) + EMBED_EPS)
    clip_unit = embedded / clip_norm
    text_unit = words / text_norm
    exact = lax.Precision.HIGHEST
    logits = (
        lax.dot_general(clip_unit, text_unit, NT, precision=exact, preferred_element_type=F32)
        / SOFTMAX_TEMP
    )
    own = lax.broadcasted_iota(jnp.int32, (n, n), 0) == lax.broadcasted_iota(
        jnp.int32, (n, n), 1
    )
    exp_logit = jnp.exp(logits)
    other = jnp.where(own, 0.0, weights)
    negative = other * exp_logit
    diagonal = jnp.where(own, logits, 0.0)
    row_self = jnp.sum(diagonal, axis=1, keepdims=True)
    col_self = jnp.sum(diagonal, axis=0, keepdims=True)
    row_weight = jnp.sum(other, axis=1, keepdims=True)
    col_weight = jnp.sum(other, axis=0, keepdims=True)
    row_part = (
        jnp.exp(row_self) + (n - 1) * jnp.sum(negative, axis=1, keepdims=True) / row_weight
    )
    col_part = (
        jnp.exp(col_self) + (n - 1) * jnp.sum(negative, axis=0, keepdims=True) / col_weight
    )
    summed = jnp.sum(jnp.log(row_part) - row_self, axis=0, keepdims=True) + jnp.sum(
        jnp.log(col_part) - col_self, axis=1, keepdims=True
    )
    loss[...] = summed / (2 * n)
    scaled = (n - 1) * weights * exp_logit
    off = scaled * (1.0 / (row_weight * row_part)) + scaled * (1.0 / (col_weight * col_part))
    on = exp_logit / row_part - 1.0 + exp_logit / col_part - 1.0
    grad = jnp.where(own, on, off)
    d_clip = (
        jnp.dot(grad, text_unit, precision=exact, preferred_element_type=F32) / SOFTMAX_TEMP
    )
    d_text = (
        lax.dot_general(grad, clip_unit, TN, precision=exact, preferred_element_type=F32)
        / SOFTMAX_TEMP
    )
    text_all = (
        d_text - text_unit * jnp.sum(text_unit * d_text, axis=-1, keepdims=True)
    ) / text_norm
    embed_all = (
        d_clip - clip_unit * jnp.sum(clip_unit * d_clip, axis=-1, keepdims=True)
    ) / clip_norm
    row = lax.broadcasted_iota(jnp.int32, (n, 1), 0)

    def mine(array):
        return jnp.concatenate(
            [
                jnp.sum(
                    jnp.where(row == first_clip + c, array, 0.0), axis=0, keepdims=True
                )
                for c in range(2)
            ],
            axis=0,
        )

    text_grad[...] = mine(text_all)
    pooled_grad = full_dot(mine(embed_all), w_emb[...], NT)
    clip_grad[...] = pooled_grad
    d_out[...] = full_dot(pooled_grad, w_out[...], NT)


def contrast(got, w_emb, w_out):
    return pl.pallas_call(
        contrast_kernel,
        out_shape=[
            jax.ShapeDtypeStruct((2, EMB), F32),
            jax.ShapeDtypeStruct((1, 1), F32),
            jax.ShapeDtypeStruct((2, D), F32),
            jax.ShapeDtypeStruct((2, D), F32),
        ],
        in_specs=[vmem()] * 3,
        out_specs=[vmem()] * 4,
        compiler_params=params(4),
        name="contrast",
    )(got, w_emb, w_out)


def backward_kernel(clips, small, clip_grad, d_out, *refs):
    nc = len(clips)
    mine = pl.ds(clips[0] * 2 * TOK, nc * 2 * TOK)
    ql, kl, vl, rq, rk, mass = (ref.at[mine] for ref in refs[:6])
    prob = refs[6].at[:, pl.ds(clips[0] * 4, nc * 4)]
    n32, istd = (ref.at[mine] for ref in refs[7:9])
    w_qkv = refs[9]
    outs = refs[10 : 10 + 4 * nc]
    ext, total, ones4, dqs, dks, dqb, dkb, dvb = refs[10 + 4 * nc :]
    rows = nc * 2 * TOK
    ones4[...] = head_blocks((QW, QW), HEAD_DIM)
    low = low_lanes((TOK, 128))
    upper = lax.broadcasted_iota(jnp.int32, (128, TOK), 0) < HEAD_DIM
    lane = lax.broadcasted_iota(jnp.int32, (1, 128), 1)

    def attend(quad):
        firsts, seconds, thirds, norms = [], [], [], []
        for n, c in enumerate(clips):
            for p in range(2):
                head = quad * 4 + 2 * p
                lanes = slice(quad * QW + p * 128, quad * QW + (p + 1) * 128)
                factor = jnp.where(lane < HEAD_DIM, small[0, head], small[0, head + 1])
                shared = {}
                for w in range(2 * n, 2 * n + 2):
                    at = slice(w * TOK, (w + 1) * TOK)
                    held = {}

                    def first(lanes=lanes, w=w, p=p, c=c, at=at, shared=shared, held=held):
                        if not shared:
                            row = d_out[c : c + 1, lanes].astype(BF16).astype(F32)
                            spread = jnp.transpose(jnp.broadcast_to(row, (TOK, 128)))
                            shared["row"] = row
                            shared["spread"] = jnp.concatenate(
                                [jnp.where(upper, spread, 0.0), jnp.where(upper, 0.0, spread)],
                                axis=1,
                            ).astype(BF16)
                        along = jnp.dot(
                            vl[at, lanes], shared["spread"], preferred_element_type=F32
                        )
                        pt = prob[quad, 2 * w + p]
                        inner = jnp.sum(pt * along, axis=0, keepdims=True)
                        held["ds"] = (pt * (along - inner)).astype(BF16)
                        dvb[at, lanes] = (mass[at, lanes] * shared["row"]).astype(BF16)

                    def second(lanes=lanes, at=at, factor=factor, held=held):
                        ds = held["ds"]
                        dk = jnp.dot(ds, split_heads(ql[at, lanes]), preferred_element_type=F32)
                        dks[at, lanes] = dk * factor
                        held["turned"] = jnp.concatenate(
                            [jnp.transpose(ds[:, :TOK]), jnp.transpose(ds[:, TOK:])], axis=1
                        )

                    def third(lanes=lanes, at=at, factor=factor, held=held):
                        dq = jnp.dot(
                            held["turned"],
                            split_heads(kl[at, lanes]),
                            preferred_element_type=F32,
                        )
                        dqs[at, lanes] = dq * factor

                    firsts.append(first)
                    seconds.append(second)
                    thirds.append(third)
            for w in range(2 * n, 2 * n + 2):
                for part in range(2):

                    def job(w=w, part=part):
                        unit, grad, inverse, done = (
                            (ql, dqs, rq, dqb),
                            (kl, dks, rk, dkb),
                        )[part]
                        at = slice(w * TOK, (w + 1) * TOK)
                        q = slice(quad * QW, (quad + 1) * QW)
                        u = unit[at, q].astype(F32)
                        g = grad[at, q]
                        inner = jnp.dot(
                            (u * g).astype(BF16), ones4[...], preferred_element_type=F32
                        )
                        done[at, q] = ((g - u * inner) * inverse[at, q]).astype(BF16)

                    norms.append(job)
        return firsts, seconds, thirds, norms

    def collect(quad):
        jobs = []
        for part in range(0, D, QW):

            def job(part=part):
                cols = slice(part, part + QW)
                got = None
                for k, grad in enumerate((dqb, dkb, dvb)):
                    term = lax.dot_general(
                        grad[:, quad * QW : (quad + 1) * QW],
                        w_qkv[cols, k * D + quad * QW : k * D + (quad + 1) * QW],
                        NT,
                        preferred_element_type=F32,
                    )
                    got = term if got is None else got + term
                total[:, cols] = got if quad == 0 else total[:, cols] + got

            jobs.append(job)
        return jobs

    units = 4 * nc
    plan = []
    for quad in range(QUADS):
        *stages, norms = attend(quad)
        start = quad * units
        for depth, stage in enumerate(stages):
            plan += spread_jobs(stage, start + depth * LAG_B, start + depth * LAG_B + units)
        done = start + 2 * LAG_B + units - 0.9
        plan += spread_jobs(norms, done, done + 1)
        plan += spread_jobs(collect(quad), done + 1, done + 1 + units)
    emit(plan)
    for n, c in enumerate(clips):
        s0, s1, s2 = shift_of(small, c)
        off0, off1 = s0 + HALO * c, s1 + HALO * c
        turn = (COLS + s2) % COLS
        base = clip_grad[c : c + 1]

        def cells(half):
            for j in range(2 * WH):
                a, b = 2 * half + j // WH, j % WH
                halves = []
                for w in range(2):
                    start = pl.multiple_of((2 * n + w) * TOK + a * (WH * WW) + b * WW, WW)
                    dn = total[pl.ds(start, WW)]
                    y = n32[pl.ds(start, WW)]
                    inv = istd[pl.ds(start, WW)][:, :1]
                    first = jnp.mean(dn, axis=-1, keepdims=True)
                    second = jnp.mean(dn * y, axis=-1, keepdims=True)
                    halves.append(base + inv * (dn - first - y * second))
                cell = pltpu.roll(jnp.concatenate(halves, axis=0), turn, 0)
                ext[n, a + off0, b + off1] = cell.astype(BF16)

        for half in range(WT // 2):
            cells(half)
        f, nf, r, nr = OWN[c]
        outs[4 * n][...] = ext[n, f : f + nf, r : r + nr]
        for k in range(3):
            f, nf, r, nr = PIECES[c][k]
            outs[4 * n + 1 + k][...] = ext[n, f : f + nf, r : r + nr]


def backward(clips, small, clip_grad, d_out, stored, w_qkv):
    nc = len(clips)
    n = nc * 2 * TOK
    shapes = ((WT, WH, COLS, D),) + PIECE_SHAPES
    return pl.pallas_call(
        partial(backward_kernel, clips),
        out_shape=[jax.ShapeDtypeStruct(s, BF16) for s in shapes * nc],
        in_specs=[smem()] + [vmem()] * 12,
        out_specs=[vmem()] * (4 * nc),
        scratch_shapes=[
            pltpu.VMEM((nc, GRID, GRID, COLS, D), BF16),
            pltpu.VMEM((n, D), F32),
            pltpu.VMEM((QW, QW), BF16),
            pltpu.VMEM((n, D), F32),
            pltpu.VMEM((n, D), F32),
            pltpu.VMEM((n, D), BF16),
            pltpu.VMEM((n, D), BF16),
            pltpu.VMEM((n, D), BF16),
        ],
        compiler_params=params(14),
        cost_estimate=pl.CostEstimate(
            flops=2 * n * D * 3 * D, bytes_accessed=16 * 2**20, transcendentals=0
        ),
        name="backward",
    )(small, clip_grad, d_out, *stored, w_qkv)


def merge_kernel(c, small, own, a, b, corner, *refs):
    out = refs[-1]
    s0, s1, _ = shift_of(small, c)
    for f in range(WT):
        for r in range(WH):
            if c == 0:
                far_f, far_r = f < HALO, r < HALO
                gone_f, gone_r = f < s0, r < s1
                at_a, at_b, at_c = (f, r - 1), (f - 1, r), (f, r)
            else:
                far_f, far_r = f >= WT - HALO, r >= WH - HALO
                gone_f, gone_r = f >= WT + s0, r >= WH + s1
                at_a, at_b, at_c = (f - 2, r), (f, r - 2), (f - 2, r - 2)
            value = own[f, r]
            if far_f and 0 <= at_a[1] < 3:
                take = jnp.logical_and(gone_f, jnp.logical_not(gone_r))
                value = jnp.where(take, a[at_a], value)
            if far_r and 0 <= at_b[0] < 3:
                take = jnp.logical_and(jnp.logical_not(gone_f), gone_r)
                value = jnp.where(take, b[at_b], value)
            if far_f and far_r:
                value = jnp.where(jnp.logical_and(gone_f, gone_r), corner[at_c], value)
            out[0, f, r] = value


def merge(clip, small, own, got, other=None):
    rest = [] if other is None else [other]
    return pl.pallas_call(
        partial(merge_kernel, clip),
        grid=(1,),
        out_shape=jax.ShapeDtypeStruct((2, WT, WH, COLS, D), BF16),
        in_specs=[smem()] + [vmem()] * 4 + [pl.BlockSpec(memory_space=pl.ANY)] * len(rest),
        out_specs=pl.BlockSpec((1, WT, WH, COLS, D), lambda i: (clip, 0, 0, 0, 0)),
        input_output_aliases={5: 0} if rest else {},
        compiler_params=params(4),
        name="merge",
    )(small, own, *got, *rest)


def local(video, shifts, head_scale, w_qkv, w_out, w_emb, text, bucket, bucket_scale):
    tokens = lax.axis_size("tm") * lax.axis_size("space") * WT * WH * COLS
    peers = lax.axis_size("batch")
    *pieces, video = pack(video)
    halo = exchange(pieces[:3], 0, -1) + exchange(pieces[3:], 1, -1)
    wide = jnp.pad(shifts.astype(F32), ((0, 0), (0, HEADS - shifts.shape[1])))
    small = jnp.concatenate([head_scale[None], wide], axis=0)
    w_qkv = load(halo[0], w_qkv)
    *stored, sums = forward(small, video, halo, w_qkv)
    spread = share(sums, w_out, w_emb, tokens)
    got = lax.all_to_all(spread, ("tm", "space"), 0, 0)
    packed = embed(got, text, bucket, bucket_scale, peers)
    got = lax.all_to_all(packed, "batch", 0, 0)
    text_grad, loss, clip_grad, d_out = contrast(got, w_emb, w_out)
    parts = []
    for c in range(2):
        mine, *pieces = backward((c,), small, clip_grad, d_out, stored, w_qkv)
        parts.append((mine, exchange(pieces, c, 1)))
    video_grad = merge(0, small, *parts[0])
    video_grad = merge(1, small, *parts[1], video_grad)
    return (video_grad, text_grad, loss[0, 0])


def solution(mesh):
    in_specs = (
        P("batch", "tm", "space", None, None),
        P("batch", None),
        P(),
        P(),
        P(),
        P(),
        P("batch", None),
        P("batch", None),
        P(),
    )
    out_specs = (P("batch", "tm", "space", None, None), P("batch", None), P())
    return jax.shard_map(local, mesh=mesh, in_specs=in_specs, out_specs=out_specs, check_vma=False)
```

```python
from functools import partial

import jax
import jax.numpy as jnp
from jax import lax
from jax.experimental import pallas as pl
from jax.experimental.pallas import tpu as pltpu
from jax.sharding import PartitionSpec as P

HEADS = 16
HEAD_DIM = 64
D = 1024
EMB = 768
WT = 4
WH = 4
WW = 8
COLS = 16
HALO = 2
TOK = WT * WH * WW
QUADS = 4
QW = 256

SOFTMAX_TEMP = 0.07
NORM_EPS = 1e-05
QUERY_EPS = 1e-06
EMBED_EPS = 1e-06
LOG2E = 1.4426950408889634
F32 = jnp.float32
BF16 = jnp.bfloat16
MIB = 1024 * 1024

NN = (((1,), (0,)), ((), ()))
NT = (((1,), (1,)), ((), ()))
TN = (((0,), (0,)), ((), ()))

GRID = 6
OWN = ((0, 4, 0, 4), (2, 4, 2, 4))
PIECES = (
    ((4, 2, 1, 3), (1, 3, 4, 2), (4, 2, 4, 2)),
    ((0, 2, 2, 3), (2, 3, 0, 2), (0, 2, 0, 2)),
)
GIVEN = (
    ((0, 2, 1, 3), (1, 3, 0, 2), (0, 2, 0, 2)),
    ((2, 2, 0, 3), (0, 3, 2, 2), (2, 2, 2, 2)),
)
PIECE_SHAPES = tuple((g[1], g[3], COLS, D) for g in GIVEN[0])


def vmem():
    return pl.BlockSpec(memory_space=pltpu.VMEM)


def smem():
    return pl.BlockSpec(memory_space=pltpu.SMEM)


def params(mib):
    return pltpu.CompilerParams(vmem_limit_bytes=mib * MIB)


def pack_kernel(video, *outs):
    for c in range(2):
        for k in range(3):
            f, nf, r, nr = GIVEN[c][k]
            outs[3 * c + k][...] = video[c, f : f + nf, r : r + nr]
    outs[6][...] = video[...]


def pack(video):
    return pl.pallas_call(
        pack_kernel,
        out_shape=[jax.ShapeDtypeStruct(s, BF16) for s in PIECE_SHAPES * 2 + (video.shape,)],
        in_specs=[vmem()],
        out_specs=[vmem()] * 7,
        compiler_params=params(4),
        name="pack",
    )(video)


def load_kernel(after, w_hbm, w_out, sem):
    copy = pltpu.make_async_copy(w_hbm, w_out, sem)
    copy.start()
    copy.wait()


def load(after, w_qkv):
    anywhere = pl.BlockSpec(memory_space=pl.ANY)
    return pl.pallas_call(
        load_kernel,
        out_shape=jax.ShapeDtypeStruct(w_qkv.shape, w_qkv.dtype),
        in_specs=[anywhere] * 2,
        out_specs=vmem(),
        scratch_shapes=[pltpu.SemaphoreType.DMA],
        compiler_params=params(4),
        cost_estimate=pl.CostEstimate(
            flops=0, bytes_accessed=4 * w_qkv.size, transcendentals=0
        ),
        name="load",
    )(after, w_qkv)


def shift_of(small, clip):
    return tuple(small[1 + clip, k].astype(jnp.int32) for k in range(3))


def exchange(pieces, clip, sign):
    tm, space = lax.axis_size("tm"), lax.axis_size("space")
    step = sign if clip == 0 else -sign
    out = []
    for piece, (dt, ds) in zip(pieces, ((step, 0), (0, step), (step, step))):
        pairs = [
            (t * space + s, ((t + dt) % tm) * space + (s + ds) % space)
            for t in range(tm)
            for s in range(space)
        ]
        out.append(lax.ppermute(piece, ("tm", "space"), pairs))
    return out


def head_blocks(shape, width):
    row = lax.broadcasted_iota(jnp.int32, shape, 0) // width
    lane = lax.broadcasted_iota(jnp.int32, shape, 1) // HEAD_DIM
    return (row == lane).astype(F32).astype(BF16)


def low_lanes(shape):
    return lax.broadcasted_iota(jnp.int32, shape, 1) < HEAD_DIM


def split_heads(pair):
    low = low_lanes((1, 2 * HEAD_DIM)).astype(F32)
    return jnp.concatenate(
        [pair * low.astype(BF16), pair * (1.0 - low).astype(BF16)], axis=0
    )


def window_mask(frame0, row0, col0, s0, s1, s2, frames, rows):
    def label(index):
        f = frame0 + index // (WH * WW) + s0
        r = row0 + (index // WW) % WH + s1
        c = col0 + index % WW + s2
        one = lambda v, n: jnp.where((v < 0) | (v >= n), 1, 0)
        return one(f, frames) * 4 + one(r, rows) * 2 + one(c, COLS)

    key = lax.broadcasted_iota(jnp.int32, (TOK, 1), 0)
    query = lax.broadcasted_iota(jnp.int32, (1, 2 * TOK), 1) % TOK
    return jnp.where(label(key) == label(query), 1.0, 0.0)


def forward_kernel(clips, frames, rows_all, small, video, *refs):
    nc = len(clips)
    frame0 = lax.axis_index("tm") * WT
    row0 = lax.axis_index("space") * WH
    halo, refs = refs[: 3 * nc], refs[3 * nc :]
    w_qkv, refs = refs[0], refs[1:]
    ql, kl, vl, rq, rk, mass, prob, n32, istd, sums = refs[:10]
    ext, xb, masks, ones4, ones2, qs, ks = refs[10:]
    ones4[...] = head_blocks((QW, QW), HEAD_DIM)
    ones2[...] = head_blocks((2 * TOK, 2 * HEAD_DIM), TOK)
    for n, c in enumerate(clips):
        f, nf, r, nr = OWN[c]
        ext[n, f : f + nf, r : r + nr] = video[c]
        for k in range(3):
            f, nf, r, nr = PIECES[c][k]
            ext[n, f : f + nf, r : r + nr] = halo[3 * n + k][...]
        s0, s1, s2 = shift_of(small, c)
        off0, off1 = s0 + HALO * c, s1 + HALO * c
        turn = (COLS - s2) % COLS

        def cells(half, total):
            for j in range(2 * WH):
                a, b = 2 * half + j // WH, j % WH
                x = ext[n, a + off0, b + off1].astype(F32)
                total = total + x
                x = pltpu.roll(x, turn, 0)
                centered = x - jnp.mean(x, axis=-1, keepdims=True)
                inv = lax.rsqrt(
                    jnp.mean(centered * centered, axis=-1, keepdims=True) + NORM_EPS
                )
                y = centered * inv
                wide = jnp.broadcast_to(inv, (COLS, 128))
                for w in range(2):
                    start = pl.multiple_of((2 * n + w) * TOK + a * (WH * WW) + b * WW, WW)
                    n32[pl.ds(start, WW)] = y[w * WW : (w + 1) * WW]
                    istd[pl.ds(start, WW)] = wide[w * WW : (w + 1) * WW]
            return total

        total = jnp.zeros((COLS, D), F32)
        for half in range(WT // 2):
            total = cells(half, total)
        sums[2 * n : 2 * n + 1] = jnp.sum(total, axis=0, keepdims=True)
        for w in range(2):
            masks[2 * n + w] = window_mask(
                frame0, row0, w * WW, s0, s1, s2, frames, rows_all
            )
    xb[...] = n32[...].astype(BF16)
    lane = lax.broadcasted_iota(jnp.int32, (1, 2 * TOK), 1)

    def project(quad):
        jobs = []
        at_quad = slice(quad * QW, (quad + 1) * QW)
        for part in range(3):

            def job(part=part):
                w = w_qkv[:, part * D + quad * QW : part * D + (quad + 1) * QW]
                value = jnp.dot(xb[...], w, preferred_element_type=F32)
                if part == 2:
                    vl[:, at_quad] = value.astype(BF16)
                else:
                    (qs, ks)[part][...] = value

            jobs.append(job)
        for part in range(2):
            for w in range(2 * nc):

                def job(part=part, w=w):
                    at = slice(w * TOK, (w + 1) * TOK)
                    full, unit, inverse = ((qs, ql, rq), (ks, kl, rk))[part]
                    value = full[at]
                    square = jnp.dot(
                        (value * value).astype(BF16), ones4[...], preferred_element_type=F32
                    )
                    inv = lax.rsqrt(square + QUERY_EPS)
                    inverse[at, at_quad] = inv
                    unit[at, at_quad] = (value * inv).astype(BF16)

                jobs.append(job)
        return jobs

    def attend(quad):
        firsts, seconds = [], []
        for p in range(2):
            head = quad * 4 + 2 * p
            lanes = slice(quad * QW + p * 128, quad * QW + (p + 1) * 128)
            for w in range(2 * nc):
                at = slice(w * TOK, (w + 1) * TOK)
                held = {}

                def first(head=head, lanes=lanes, w=w, at=at, p=p, held=held):
                    factor = jnp.where(lane < TOK, small[0, head], small[0, head + 1]) * LOG2E
                    score = lax.dot_general(
                        kl[at, lanes], split_heads(ql[at, lanes]), NT, preferred_element_type=F32
                    )
                    e = jnp.exp2(score * factor) * masks[w]
                    held["e"] = e
                    held["inv"] = 1.0 / jnp.sum(e, axis=0, keepdims=True)

                def second(lanes=lanes, w=w, at=at, p=p, held=held):
                    pt = held["e"] * held["inv"]
                    prob[quad, 2 * w + p] = pt
                    mass_here = jnp.dot(pt.astype(BF16), ones2[...], preferred_element_type=F32)
                    mass[at, lanes] = mass_here
                    gathered = jnp.sum(
                        mass_here * vl[at, lanes].astype(F32), axis=0, keepdims=True
                    )
                    row = slice(w // 2 * 2 + 1, w // 2 * 2 + 2)
                    if w % 2:
                        sums[row, lanes] = sums[row, lanes] + gathered
                    else:
                        sums[row, lanes] = gathered

                firsts.append(first)
                seconds.append(second)
        return firsts, seconds

    units = 4 * nc
    plan = spread_jobs(project(0), -1, 0)
    for quad in range(QUADS):
        start = quad * units
        for depth, stage in enumerate(attend(quad)):
            plan += spread_jobs(stage, start + depth * LAG_F, start + depth * LAG_F + units)
        if quad + 1 < QUADS:
            plan += spread_jobs(project(quad + 1), start, start + units - 0.1)
    emit(plan)


LAG_F = 3
LAG_B = 2


def spread_jobs(jobs, start, end):
    step = (end - start) / len(jobs)
    return [(start + k * step, job) for k, job in enumerate(jobs)]


def emit(plan):
    for _, job in sorted(plan, key=lambda item: item[0]):
        job()


def forward(small, video, halo, w_qkv):
    clips = (0, 1)
    nc = len(clips)
    n = nc * 2 * TOK
    frames = lax.axis_size("tm") * WT
    rows_all = lax.axis_size("space") * WH
    return pl.pallas_call(
        partial(forward_kernel, clips, frames, rows_all),
        out_shape=[jax.ShapeDtypeStruct((n, D), BF16)] * 3
        + [jax.ShapeDtypeStruct((n, D), F32)] * 3
        + [
            jax.ShapeDtypeStruct((QUADS, 4 * nc, TOK, 2 * TOK), F32),
            jax.ShapeDtypeStruct((n, D), F32),
            jax.ShapeDtypeStruct((n, 128), F32),
            jax.ShapeDtypeStruct((2 * nc, D), F32),
        ],
        in_specs=[smem()] + [vmem()] * (2 + 3 * nc),
        out_specs=[vmem()] * 10,
        scratch_shapes=[
            pltpu.VMEM((nc, GRID, GRID, COLS, D), BF16),
            pltpu.VMEM((n, D), BF16),
            pltpu.VMEM((2 * nc, TOK, 2 * TOK), F32),
            pltpu.VMEM((QW, QW), BF16),
            pltpu.VMEM((2 * TOK, 2 * HEAD_DIM), BF16),
            pltpu.VMEM((n, QW), F32),
            pltpu.VMEM((n, QW), F32),
        ],
        compiler_params=params(12),
        cost_estimate=pl.CostEstimate(
            flops=2 * n * D * 3 * D, bytes_accessed=12 * 2**20, transcendentals=n * 2048
        ),
        name="forward",
    )(small, video, *halo, w_qkv)


def share_kernel(tokens, sums, w_out, w_emb, out):
    means = sums[...] / tokens
    pooled = jnp.concatenate([means[0:1], means[2:3]], axis=0) + full_dot(
        jnp.concatenate([means[1:2], means[3:4]], axis=0), w_out[...], NN
    )
    block = full_dot(pooled, w_emb[...], NN)
    for peer in range(out.shape[0]):
        out[peer] = block


def share(sums, w_out, w_emb, tokens):
    plane = lax.axis_size("tm") * lax.axis_size("space")
    return pl.pallas_call(
        partial(share_kernel, tokens),
        out_shape=jax.ShapeDtypeStruct((plane, 2, EMB), F32),
        in_specs=[vmem()] * 3,
        out_specs=vmem(),
        compiler_params=params(4),
        name="share",
    )(sums, w_out, w_emb)


def embed_kernel(got, text, bucket, levels, out):
    embedded = jnp.sum(got[...], axis=0)
    held = bucket[...]
    weight = jnp.zeros(held.shape, F32)
    for level in range(levels.shape[0]):
        weight = weight + jnp.where(held == level, levels[level], 0.0)
    weight = jnp.concatenate(
        [weight, jnp.zeros((held.shape[0], 128 - held.shape[1]), F32)], axis=1
    )
    words = text[...].astype(F32)
    block = jnp.concatenate(
        [
            jnp.concatenate([embedded, weight], axis=1),
            jnp.concatenate([words, jnp.zeros_like(weight)], axis=1),
        ],
        axis=0,
    )
    for peer in range(out.shape[0]):
        out[peer] = block


def embed(got, text, bucket, levels, peers):
    return pl.pallas_call(
        embed_kernel,
        out_shape=jax.ShapeDtypeStruct((peers, 4, EMB + 128), F32),
        in_specs=[vmem()] * 3 + [smem()],
        out_specs=vmem(),
        compiler_params=params(4),
        name="embed",
    )(got, text, bucket, levels)


def three_parts(wide):
    high = wide.astype(BF16)
    rest = wide - high.astype(F32)
    middle = rest.astype(BF16)
    low = (rest - middle.astype(F32)).astype(BF16)
    return jnp.concatenate([high, middle, low], axis=0)


def full_dot(wide, weight, dims):
    n = wide.shape[0]
    got = lax.dot_general(three_parts(wide), weight, dims, preferred_element_type=F32)
    return got[:n] + got[n : 2 * n] + got[2 * n :]


def own_rows(first_clip, array):
    row = lax.broadcasted_iota(jnp.int32, (array.shape[0], 1), 0)
    return jnp.concatenate(
        [
            jnp.sum(jnp.where(row == first_clip + c, array, 0.0), axis=0, keepdims=True)
            for c in range(2)
        ],
        axis=0,
    )


def caption_kernel(after, got, grad, clip_unit, out):
    peers = got.shape[0]
    words = jnp.concatenate([got[p, 2:4, :EMB] for p in range(peers)], axis=0)
    text_norm = jnp.sqrt(jnp.sum(words * words, axis=-1, keepdims=True) + EMBED_EPS)
    text_unit = words / text_norm
    d_text = (
        lax.dot_general(
            grad[...],
            clip_unit[...],
            TN,
            precision=lax.Precision.HIGHEST,
            preferred_element_type=F32,
        )
        / SOFTMAX_TEMP
    )
    text_all = (
        d_text - text_unit * jnp.sum(text_unit * d_text, axis=-1, keepdims=True)
    ) / text_norm
    out[...] = own_rows(2 * lax.axis_index("batch"), text_all)


def caption(after, got, grad, clip_unit):
    return pl.pallas_call(
        caption_kernel,
        out_shape=jax.ShapeDtypeStruct((2, EMB), F32),
        in_specs=[pl.BlockSpec(memory_space=pl.ANY)] + [vmem()] * 3,
        out_specs=vmem(),
        compiler_params=params(4),
        name="caption",
    )(after, got, grad, clip_unit)


def contrast_kernel(got, w_emb, w_out, loss, clip_grad, d_out, grad_out, clip_out):
    peers = got.shape[0]
    n = 2 * peers
    first_clip = 2 * lax.axis_index("batch")
    embedded = jnp.concatenate([got[p, 0:2, :EMB] for p in range(peers)], axis=0)
    weights = jnp.concatenate([got[p, 0:2, EMB:] for p in range(peers)], axis=0)[:, :n]
    words = jnp.concatenate([got[p, 2:4, :EMB] for p in range(peers)], axis=0)
    clip_norm = jnp.sqrt(jnp.sum(embedded * embedded, axis=-1, keepdims=True) + EMBED_EPS)
    text_norm = jnp.sqrt(jnp.sum(words * words, axis=-1, keepdims=True) + EMBED_EPS)
    clip_unit = embedded / clip_norm
    text_unit = words / text_norm
    exact = lax.Precision.HIGHEST
    logits = (
        lax.dot_general(clip_unit, text_unit, NT, precision=exact, preferred_element_type=F32)
        / SOFTMAX_TEMP
    )
    own = lax.broadcasted_iota(jnp.int32, (n, n), 0) == lax.broadcasted_iota(
        jnp.int32, (n, n), 1
    )
    exp_logit = jnp.exp(logits)
    other = jnp.where(own, 0.0, weights)
    negative = other * exp_logit
    diagonal = jnp.where(own, logits, 0.0)
    row_self = jnp.sum(diagonal, axis=1, keepdims=True)
    col_self = jnp.sum(diagonal, axis=0, keepdims=True)
    row_weight = jnp.sum(other, axis=1, keepdims=True)
    col_weight = jnp.sum(other, axis=0, keepdims=True)
    row_part = (
        jnp.exp(row_self) + (n - 1) * jnp.sum(negative, axis=1, keepdims=True) / row_weight
    )
    col_part = (
        jnp.exp(col_self) + (n - 1) * jnp.sum(negative, axis=0, keepdims=True) / col_weight
    )
    summed = jnp.sum(jnp.log(row_part) - row_self, axis=0, keepdims=True) + jnp.sum(
        jnp.log(col_part) - col_self, axis=1, keepdims=True
    )
    loss[...] = summed / (2 * n)
    scaled = (n - 1) * weights * exp_logit
    off = scaled * (1.0 / (row_weight * row_part)) + scaled * (1.0 / (col_weight * col_part))
    on = exp_logit / row_part - 1.0 + exp_logit / col_part - 1.0
    grad = jnp.where(own, on, off)
    d_clip = (
        jnp.dot(grad, text_unit, precision=exact, preferred_element_type=F32) / SOFTMAX_TEMP
    )
    grad_out[...] = grad
    clip_out[...] = clip_unit
    embed_all = (
        d_clip - clip_unit * jnp.sum(clip_unit * d_clip, axis=-1, keepdims=True)
    ) / clip_norm
    mine = partial(own_rows, first_clip)
    pooled_grad = full_dot(mine(embed_all), w_emb[...], NT)
    clip_grad[...] = pooled_grad
    d_out[...] = full_dot(pooled_grad, w_out[...], NT)


def contrast(got, w_emb, w_out):
    n = 2 * got.shape[0]
    return pl.pallas_call(
        contrast_kernel,
        out_shape=[
            jax.ShapeDtypeStruct((1, 1), F32),
            jax.ShapeDtypeStruct((2, D), F32),
            jax.ShapeDtypeStruct((2, D), F32),
            jax.ShapeDtypeStruct((n, n), F32),
            jax.ShapeDtypeStruct((n, EMB), F32),
        ],
        in_specs=[vmem()] * 3,
        out_specs=[vmem()] * 5,
        compiler_params=params(4),
        name="contrast",
    )(got, w_emb, w_out)


def backward_kernel(clips, small, clip_grad, d_out, *refs):
    nc = len(clips)
    mine = pl.ds(clips[0] * 2 * TOK, nc * 2 * TOK)
    ql, kl, vl, rq, rk, mass = (ref.at[mine] for ref in refs[:6])
    prob = refs[6].at[:, pl.ds(clips[0] * 4, nc * 4)]
    n32, istd = (ref.at[mine] for ref in refs[7:9])
    w_qkv = refs[9]
    outs = refs[10 : 10 + 4 * nc]
    ext, total, ones4, dqs, dks, dqb, dkb, dvb = refs[10 + 4 * nc :]
    rows = nc * 2 * TOK
    ones4[...] = head_blocks((QW, QW), HEAD_DIM)
    low = low_lanes((TOK, 128))
    upper = lax.broadcasted_iota(jnp.int32, (128, TOK), 0) < HEAD_DIM
    lane = lax.broadcasted_iota(jnp.int32, (1, 128), 1)

    def attend(quad):
        firsts, seconds, thirds, norms = [], [], [], []
        for n, c in enumerate(clips):
            for p in range(2):
                head = quad * 4 + 2 * p
                lanes = slice(quad * QW + p * 128, quad * QW + (p + 1) * 128)
                factor = jnp.where(lane < HEAD_DIM, small[0, head], small[0, head + 1])
                shared = {}
                for w in range(2 * n, 2 * n + 2):
                    at = slice(w * TOK, (w + 1) * TOK)
                    held = {}

                    def first(lanes=lanes, w=w, p=p, c=c, at=at, shared=shared, held=held):
                        if not shared:
                            row = d_out[c : c + 1, lanes].astype(BF16).astype(F32)
                            spread = jnp.transpose(jnp.broadcast_to(row, (TOK, 128)))
                            shared["row"] = row
                            shared["spread"] = jnp.concatenate(
                                [jnp.where(upper, spread, 0.0), jnp.where(upper, 0.0, spread)],
                                axis=1,
                            ).astype(BF16)
                        along = jnp.dot(
                            vl[at, lanes], shared["spread"], preferred_element_type=F32
                        )
                        pt = prob[quad, 2 * w + p]
                        inner = jnp.sum(pt * along, axis=0, keepdims=True)
                        held["ds"] = (pt * (along - inner)).astype(BF16)
                        dvb[at, lanes] = (mass[at, lanes] * shared["row"]).astype(BF16)

                    def second(lanes=lanes, at=at, factor=factor, held=held):
                        ds = held["ds"]
                        dk = jnp.dot(ds, split_heads(ql[at, lanes]), preferred_element_type=F32)
                        dks[at, lanes] = dk * factor
                        held["turned"] = jnp.concatenate(
                            [jnp.transpose(ds[:, :TOK]), jnp.transpose(ds[:, TOK:])], axis=1
                        )

                    def third(lanes=lanes, at=at, factor=factor, held=held):
                        dq = jnp.dot(
                            held["turned"],
                            split_heads(kl[at, lanes]),
                            preferred_element_type=F32,
                        )
                        dqs[at, lanes] = dq * factor

                    firsts.append(first)
                    seconds.append(second)
                    thirds.append(third)
            for w in range(2 * n, 2 * n + 2):
                for part in range(2):

                    def job(w=w, part=part):
                        unit, grad, inverse, done = (
                            (ql, dqs, rq, dqb),
                            (kl, dks, rk, dkb),
                        )[part]
                        at = slice(w * TOK, (w + 1) * TOK)
                        q = slice(quad * QW, (quad + 1) * QW)
                        u = unit[at, q].astype(F32)
                        g = grad[at, q]
                        inner = jnp.dot(
                            (u * g).astype(BF16), ones4[...], preferred_element_type=F32
                        )
                        done[at, q] = ((g - u * inner) * inverse[at, q]).astype(BF16)

                    norms.append(job)
        return firsts, seconds, thirds, norms

    def collect(quad):
        jobs = []
        for part in range(0, D, QW):

            def job(part=part):
                cols = slice(part, part + QW)
                got = None
                for k, grad in enumerate((dqb, dkb, dvb)):
                    term = lax.dot_general(
                        grad[:, quad * QW : (quad + 1) * QW],
                        w_qkv[cols, k * D + quad * QW : k * D + (quad + 1) * QW],
                        NT,
                        preferred_element_type=F32,
                    )
                    got = term if got is None else got + term
                total[:, cols] = got if quad == 0 else total[:, cols] + got

            jobs.append(job)
        return jobs

    units = 4 * nc
    plan = []
    for quad in range(QUADS):
        *stages, norms = attend(quad)
        start = quad * units
        for depth, stage in enumerate(stages):
            plan += spread_jobs(stage, start + depth * LAG_B, start + depth * LAG_B + units)
        done = start + 2 * LAG_B + units - 0.9
        plan += spread_jobs(norms, done, done + 1)
        plan += spread_jobs(collect(quad), done + 1, done + 1 + units)
    emit(plan)
    for n, c in enumerate(clips):
        s0, s1, s2 = shift_of(small, c)
        off0, off1 = s0 + HALO * c, s1 + HALO * c
        turn = (COLS + s2) % COLS
        base = clip_grad[c : c + 1]

        def cells(half):
            for j in range(2 * WH):
                a, b = 2 * half + j // WH, j % WH
                halves = []
                for w in range(2):
                    start = pl.multiple_of((2 * n + w) * TOK + a * (WH * WW) + b * WW, WW)
                    dn = total[pl.ds(start, WW)]
                    y = n32[pl.ds(start, WW)]
                    inv = istd[pl.ds(start, WW)][:, :1]
                    first = jnp.mean(dn, axis=-1, keepdims=True)
                    second = jnp.mean(dn * y, axis=-1, keepdims=True)
                    halves.append(base + inv * (dn - first - y * second))
                cell = pltpu.roll(jnp.concatenate(halves, axis=0), turn, 0)
                ext[n, a + off0, b + off1] = cell.astype(BF16)

        for half in range(WT // 2):
            cells(half)
        f, nf, r, nr = OWN[c]
        outs[4 * n][...] = ext[n, f : f + nf, r : r + nr]
        for k in range(3):
            f, nf, r, nr = PIECES[c][k]
            outs[4 * n + 1 + k][...] = ext[n, f : f + nf, r : r + nr]


def backward(clips, small, clip_grad, d_out, stored, w_qkv):
    nc = len(clips)
    n = nc * 2 * TOK
    shapes = ((WT, WH, COLS, D),) + PIECE_SHAPES
    return pl.pallas_call(
        partial(backward_kernel, clips),
        out_shape=[jax.ShapeDtypeStruct(s, BF16) for s in shapes * nc],
        in_specs=[smem()] + [vmem()] * 12,
        out_specs=[vmem()] * (4 * nc),
        scratch_shapes=[
            pltpu.VMEM((nc, GRID, GRID, COLS, D), BF16),
            pltpu.VMEM((n, D), F32),
            pltpu.VMEM((QW, QW), BF16),
            pltpu.VMEM((n, D), F32),
            pltpu.VMEM((n, D), F32),
            pltpu.VMEM((n, D), BF16),
            pltpu.VMEM((n, D), BF16),
            pltpu.VMEM((n, D), BF16),
        ],
        compiler_params=params(14),
        cost_estimate=pl.CostEstimate(
            flops=2 * n * D * 3 * D, bytes_accessed=16 * 2**20, transcendentals=0
        ),
        name="backward",
    )(small, clip_grad, d_out, *stored, w_qkv)


def merge_kernel(c, small, own, a, b, corner, *refs):
    out = refs[-1]
    s0, s1, _ = shift_of(small, c)
    for f in range(WT):
        for r in range(WH):
            if c == 0:
                far_f, far_r = f < HALO, r < HALO
                gone_f, gone_r = f < s0, r < s1
                at_a, at_b, at_c = (f, r - 1), (f - 1, r), (f, r)
            else:
                far_f, far_r = f >= WT - HALO, r >= WH - HALO
                gone_f, gone_r = f >= WT + s0, r >= WH + s1
                at_a, at_b, at_c = (f - 2, r), (f, r - 2), (f - 2, r - 2)
            value = own[f, r]
            if far_f and 0 <= at_a[1] < 3:
                take = jnp.logical_and(gone_f, jnp.logical_not(gone_r))
                value = jnp.where(take, a[at_a], value)
            if far_r and 0 <= at_b[0] < 3:
                take = jnp.logical_and(jnp.logical_not(gone_f), gone_r)
                value = jnp.where(take, b[at_b], value)
            if far_f and far_r:
                value = jnp.where(jnp.logical_and(gone_f, gone_r), corner[at_c], value)
            out[0, f, r] = value


def merge(clip, small, own, got, other=None):
    rest = [] if other is None else [other]
    return pl.pallas_call(
        partial(merge_kernel, clip),
        grid=(1,),
        out_shape=jax.ShapeDtypeStruct((2, WT, WH, COLS, D), BF16),
        in_specs=[smem()] + [vmem()] * 4 + [pl.BlockSpec(memory_space=pl.ANY)] * len(rest),
        out_specs=pl.BlockSpec((1, WT, WH, COLS, D), lambda i: (clip, 0, 0, 0, 0)),
        input_output_aliases={5: 0} if rest else {},
        compiler_params=params(4),
        name="merge",
    )(small, own, *got, *rest)


def local(video, shifts, head_scale, w_qkv, w_out, w_emb, text, bucket, bucket_scale):
    tokens = lax.axis_size("tm") * lax.axis_size("space") * WT * WH * COLS
    peers = lax.axis_size("batch")
    *pieces, video = pack(video)
    halo = exchange(pieces[:3], 0, -1) + exchange(pieces[3:], 1, -1)
    wide = jnp.pad(shifts.astype(F32), ((0, 0), (0, HEADS - shifts.shape[1])))
    small = jnp.concatenate([head_scale[None], wide], axis=0)
    w_qkv = load(halo[0], w_qkv)
    *stored, sums = forward(small, video, halo, w_qkv)
    spread = share(sums, w_out, w_emb, tokens)
    got = lax.all_to_all(spread, ("tm", "space"), 0, 0)
    packed = embed(got, text, bucket, bucket_scale, peers)
    got = lax.all_to_all(packed, "batch", 0, 0)
    loss, clip_grad, d_out, grad, clip_unit = contrast(got, w_emb, w_out)
    parts = []
    for c in range(2):
        mine, *pieces = backward((c,), small, clip_grad, d_out, stored, w_qkv)
        parts.append((mine, exchange(pieces, c, 1)))
    text_grad = caption(parts[0][1][0], got, grad, clip_unit)
    video_grad = merge(0, small, *parts[0])
    video_grad = merge(1, small, *parts[1], video_grad)
    return (video_grad, text_grad, loss[0, 0])


def solution(mesh):
    in_specs = (
        P("batch", "tm", "space", None, None),
        P("batch", None),
        P(),
        P(),
        P(),
        P(),
        P("batch", None),
        P("batch", None),
        P(),
    )
    out_specs = (P("batch", "tm", "space", None, None), P("batch", None), P())
    return jax.shard_map(local, mesh=mesh, in_specs=in_specs, out_specs=out_specs, check_vma=False)
```
